32 devices in a mesh: rows: 8 (over z, y), cols: 4 (over x, core).
Axes of the slice: x: 2, y: 2, z: 4, core: 2. Of those that a mesh axis runs over, the one named last changes fastest.
Arguments:
- embeddings: bfloat16 [8192, 1024], P('rows'), may hold values from -6 to 6
- knn_mean: bfloat16 [8192], P('rows'), may hold values from 0.29882812 to 0.8984375
- pair_rows: int32 [8, 4, 24], P('rows', 'cols'), may hold values from 0 to 31, as said below
- pair_cols: int32 [8, 4, 24], P('rows', 'cols'), may hold values from 0 to 31, as said below
- pair_count: int32 [8, 4], P('rows', 'cols'), may hold values from 2 to 24, as said below
- start_block: float32 [64, 8192], P(None, 'rows')
Outputs:
- block_vector: float32 [64, 8192], P(None, 'rows')
The draws below stay inside these ranges and needn't reach their ends.
Inputs may be any that keep to these rules, and one draw needn't show every extreme that they name: `pair_count`: on every index of rows one device of cols has exactly 24 live slots. `pair_rows`: A live entry of device (i, j) is one of the row blocks i * 4 to (i + 1) * 4 - 1; the live pairs of one index of rows are all different, and each of its row blocks is paired with itself. Slots at pair_count and beyond are unused and repeat the device's first pair. `pair_cols`: the column block of a live pair of device (i, j) is a row block of rows index i - 1, i or i + 1.
All inputs are finite; a program needn't handle non-finite values.
Results may differ from the reference program's by a relative error of at most 0.0065.
Values may be sent and summed in bfloat16 or wider, within the bound.
No kernel may reach another device: no remote copies, remote signals or barrier semaphores. Data moves between devices by JAX's collectives and lax.ppermute only.
A program may use at most 64 MiB of HBM per device.

```python
import math
import jax
import jax.numpy as jnp
from jax import lax

E = 1024
K = 64
BLOCK = 256
BLK_DEV = 4
ITERS = 2
PAIRS_DEV = 24
SENTENCES = 8192
N_ROWS = 8
N_COLS = 4


def pair_tables(key):
    base = jax.random.fold_in(key, 4242)
    key_count, key_full, key_order = jax.random.split(base, 3)
    span = 3 * BLK_DEV
    number = BLK_DEV * span
    index = jnp.arange(number, dtype=jnp.int32)
    row_local = index // span
    window = index % span
    groups = jnp.arange(N_ROWS, dtype=jnp.int32)[:, None]
    column = (groups - 1) * BLK_DEV + window[None, :]
    valid = (column >= 0) & (column < N_ROWS * BLK_DEV)
    valid_count = jnp.sum(valid.astype(jnp.int32), axis=1)
    room = (valid_count - PAIRS_DEV) // (N_COLS - 1)
    counts = jax.random.randint(key_count, (N_ROWS, N_COLS), BLK_DEV, 3 * BLK_DEV, dtype=jnp.int32)
    counts = jnp.maximum(jnp.minimum(counts, room[:, None]), 2)
    full = jax.random.randint(key_full, (N_ROWS,), 0, N_COLS, dtype=jnp.int32)
    lanes = jnp.arange(N_COLS, dtype=jnp.int32)
    counts = jnp.where(lanes[None, :] == full[:, None], jnp.int32(PAIRS_DEV), counts)
    diagonal = window == row_local + BLK_DEV
    noise = jax.random.randint(key_order, (N_ROWS, number), 0, 65536, dtype=jnp.int32)
    score = noise * number + index[None, :] + number
    score = jnp.where(diagonal[None, :], jnp.broadcast_to(index[None, :], score.shape), score)
    score = jnp.where(valid, score, score + 268435456)
    order = jnp.argsort(score, axis=1).astype(jnp.int32)
    offsets = jnp.cumsum(counts, axis=1) - counts
    slots = jnp.arange(PAIRS_DEV, dtype=jnp.int32)
    position = offsets[:, :, None] + slots[None, None, :]
    position = jnp.where(slots[None, None, :] < counts[:, :, None], position, jnp.broadcast_to(offsets[:, :, None], position.shape))
    chosen = jnp.take_along_axis(jnp.broadcast_to(order[:, None, :], (N_ROWS, N_COLS, number)), position, axis=2)
    rows_out = groups[:, :, None] * BLK_DEV + chosen // span
    cols_out = (groups[:, :, None] - 1) * BLK_DEV + chosen % span
    return (rows_out.astype(jnp.int32), cols_out.astype(jnp.int32), counts.astype(jnp.int32))


def draw_pair_rows(key, part):
    return pair_tables(key)[0]


def draw_pair_cols(key, part):
    return pair_tables(key)[1]


def draw_pair_count(key, part):
    return pair_tables(key)[2]


def draw_start_block(key, part):
    place = jnp.arange(SENTENCES, dtype=jnp.float32) / SENTENCES
    rising = jnp.exp(math.log(3.0) * place)[None, :]
    result = jax.random.normal(key, (K, SENTENCES), jnp.float32) * rising
    return result.astype(jnp.float32)


def steps_of(stream_key, dims, cuts, least, top_value):
    factor_of, own = 1.0, jax.random.fold_in(stream_key, 6)
    for dim, blocks in cuts:
        draws = jnp.exp(jax.random.uniform(jax.random.fold_in(own, dim), (blocks,), jnp.float32, least / len(cuts), top_value / len(cuts)))
        factor_of = factor_of * jnp.repeat(draws, dims[dim] // blocks).reshape([-1 if axis == dim else 1 for axis in range(len(dims))])
    return factor_of


def gaussian(stream_key, shape, spread, bound, cuts=(), kind=jnp.bfloat16):
    drawn = spread * jax.random.normal(stream_key, shape, jnp.float32)
    if cuts:
        drawn = drawn * steps_of(stream_key, shape, cuts, -0.22, 0.18)
    return jnp.clip(drawn, -bound, bound).astype(kind)


def setup_inputs(seed: int = 0) -> dict:
    splits = jax.random.split(jax.random.key(seed), 7)
    return {
        "embeddings": gaussian(splits[0], (SENTENCES, E), 1.0, 6.0, ((0, 8),)),
        "knn_mean": jnp.clip(jnp.exp(math.log(0.8984375) - 1.1007886 * jax.random.uniform(splits[1], (SENTENCES,), jnp.float32) ** steps_of(splits[1], (SENTENCES,), ((0, 8),), -0.2, 0.2)), 0.29882812, 0.8984375).astype(jnp.bfloat16),
        "pair_rows": draw_pair_rows(jax.random.fold_in(splits[6], 71), 0),
        "pair_cols": draw_pair_cols(jax.random.fold_in(splits[6], 71), 0),
        "pair_count": draw_pair_count(jax.random.fold_in(splits[6], 71), 0),
        "start_block": draw_start_block(jax.random.fold_in(splits[6], 71), 0),
    }


sharpness = 10.0
epsilon = 1e-06

def unit_rows(embeddings):
    values = embeddings.astype(jnp.float32)
    scale = lax.rsqrt(lax.optimization_barrier(jnp.mean(values * values, axis=1, keepdims=True)) + epsilon)
    return (values * scale / math.sqrt(values.shape[1])).astype(jnp.bfloat16)

def make_affinity(row_unit, col_unit, row_mean, col_mean, row_block, col_block):
    size = row_unit.shape[0]
    scores = lax.dot_general(row_unit.astype(jnp.float32), col_unit.astype(jnp.float32), (((1,), (1,)), ((), ())), preferred_element_type=jnp.float32)
    denom = 0.5 * (row_mean.astype(jnp.float32)[:, None] + col_mean.astype(jnp.float32)[None, :])
    weights = jnp.exp(sharpness * scores / denom)
    offsets = jnp.arange(size, dtype=jnp.int32)
    same = (row_block * size + offsets)[:, None] == (col_block * size + offsets)[None, :]
    return jnp.where(same, jnp.zeros_like(weights), weights).astype(jnp.bfloat16)

def add_block(accum, piece, block_index):
    size = piece.shape[1]
    current = lax.dynamic_slice_in_dim(accum, block_index * size, size, 1)
    return lax.dynamic_update_slice_in_dim(accum, current + piece, block_index * size, 1)

def reference(embeddings, knn_mean, pair_rows, pair_cols, pair_count, start_block):
    unit = unit_rows(embeddings)
    slots = pair_rows.shape[2]
    live = (jnp.arange(slots, dtype=jnp.int32)[None, None, :] < pair_count[:, :, None]).reshape(-1)
    flat_rows = pair_rows.reshape(-1).astype(jnp.int32)
    flat_cols = pair_cols.reshape(-1).astype(jnp.int32)
    total_rows = embeddings.shape[0]
    vector = start_block
    for sweep in range(ITERS):
        narrow = vector.astype(jnp.bfloat16)

        def accumulate(state, item):
            row_block, col_block, active = item

            def apply(inner):
                vector_acc, degree_acc = inner
                row_unit = lax.dynamic_slice_in_dim(unit, row_block * BLOCK, BLOCK, 0)
                col_unit = lax.dynamic_slice_in_dim(unit, col_block * BLOCK, BLOCK, 0)
                row_mean = lax.dynamic_slice_in_dim(knn_mean, row_block * BLOCK, BLOCK, 0)
                col_mean = lax.dynamic_slice_in_dim(knn_mean, col_block * BLOCK, BLOCK, 0)
                affinity = make_affinity(row_unit, col_unit, row_mean, col_mean, row_block, col_block)
                degree_acc = add_block(degree_acc, lax.optimization_barrier(jnp.sum(affinity.astype(jnp.float32), axis=1))[None, :], row_block)
                source = lax.dynamic_slice_in_dim(narrow, col_block * BLOCK, BLOCK, 1)
                product = lax.dot_general(source.astype(jnp.float32), affinity.astype(jnp.float32), (((1,), (1,)), ((), ())), preferred_element_type=jnp.float32)
                vector_acc = add_block(vector_acc, product, row_block)
                return (vector_acc, degree_acc)
            return (lax.cond(active, apply, lambda inner: inner, state), None)
        init = (jnp.zeros((K, total_rows), jnp.float32), jnp.zeros((1, total_rows), jnp.float32))
        (summed, degree), _ = lax.scan(accumulate, init, (flat_rows, flat_cols, live))
        smoothed = summed / degree
        gram = jnp.dot(smoothed.astype(jnp.float32), smoothed.T.astype(jnp.float32), precision=lax.Precision.HIGHEST, preferred_element_type=jnp.float32) / total_rows
        lower = jnp.linalg.cholesky(gram)
        vector = jax.scipy.linalg.solve_triangular(lower, smoothed, lower=True)
    return vector
```

```python
import functools
import math

import jax
import jax.numpy as jnp
from jax import lax
from jax.experimental import pallas as pl
from jax.experimental.pallas import tpu as pltpu
from jax.sharding import PartitionSpec as P

BLOCK = 256
ONES = 16

sharpness = 10.0
epsilon = 1e-06

HIGHEST = lax.Precision.HIGHEST
f32 = jnp.float32
bf16 = jnp.bfloat16


def shift(cells, step):
    count = lax.axis_size("rows")
    return lax.ppermute(cells, "rows", [(i, (i + step) % count) for i in range(count)])


def swap(cells, axis, offset):
    count = lax.axis_size(axis)
    return lax.ppermute(cells, axis, [(i, i ^ offset) for i in range(count)])


def lane_swaps(cells):
    return [cells] + [swap(cells, "cols", d) for d in range(1, lax.axis_size("cols"))]


def row_stages(count):
    bits = count.bit_length() - 1
    stages = []
    low = 0
    while low < bits:
        wide = 1 if (bits - low) % 2 else 2
        stages.append([m << low for m in range(1, 1 << wide)])
        low += wide
    return stages


def nt(left, right):
    return lax.dot_general(left, right, (((1,), (1,)), ((), ())), preferred_element_type=f32)


def unit_rows(cells):
    values = cells.astype(f32)
    scale = lax.rsqrt(jnp.mean(values * values, axis=1, keepdims=True) + epsilon)
    return (values * (scale * (1.0 / math.sqrt(cells.shape[1])))).astype(bf16)


def diagonal(size):
    return lax.broadcasted_iota(jnp.int32, (size, size), 0) == lax.broadcasted_iota(
        jnp.int32, (size, size), 1
    )


def upright(row, eye):
    return jnp.sum(jnp.where(eye, row, 0.0), axis=1, keepdims=True)


def affinity(col_unit, row_unit, col_mean, row_mean):
    scores = nt(col_unit, row_unit)
    return jnp.exp((2.0 * sharpness) * scores / (col_mean + row_mean))


def with_ones(narrow):
    return jnp.concatenate([narrow, jnp.ones((ONES, narrow.shape[1]), bf16)], axis=0)


def pieces(values):
    first = values.astype(bf16)
    rest = values - first.astype(f32)
    second = rest.astype(bf16)
    third = (rest - second.astype(f32)).astype(bf16)
    return jnp.concatenate([first, second, third], axis=0)


def joined(product, size):
    return product[:size] + (product[size : 2 * size] + product[2 * size :])


def inverse_factor(gram):
    size = gram.shape[0]
    eye = jnp.where(diagonal(size), 1.0, 0.0).astype(f32)
    table = jnp.concatenate([gram, eye], axis=1)
    tile = 8
    parts = [table[g * tile : (g + 1) * tile] for g in range(size // tile)]
    inner = lax.broadcasted_iota(jnp.int32, (tile, 1), 0)
    scales = []
    for k in range(size):
        home, at = k // tile, k % tile
        row = parts[home][at : at + 1]
        pivot = row[:, k : k + 1]
        scales.append(lax.rsqrt(pivot))
        row_scaled = row / pivot
        for g in range(home, size // tile):
            column = parts[g][:, k : k + 1]
            if g == home:
                column = jnp.where(inner > at, column, 0.0)
            parts[g] = parts[g] - column * row_scaled
    out = []
    for g in range(size // tile):
        scale = jnp.concatenate(scales[g * tile : (g + 1) * tile], axis=0)
        out.append(parts[g][:, size:] * scale)
    return jnp.concatenate(out, axis=0)


def times(left, right):
    return jnp.dot(left, right, precision=HIGHEST, preferred_element_type=f32)


def gram_of(blocks, total):
    acc = None
    for block in blocks:
        term = lax.dot_general(
            block, block, (((1,), (1,)), ((), ())), precision=HIGHEST, preferred_element_type=f32
        )
        acc = term if acc is None else acc + term
    return acc * (1.0 / total)


def block_of(lane, d):
    return pl.ds(pl.multiple_of((lane ^ d) * BLOCK, BLOCK), BLOCK)


def own_kernel(lanes, cells_ref, mean_ref, start_ref, unit_ref, weight_ref, product_ref):
    lane = lax.axis_index("cols")
    for d in range(lanes):
        unit_ref[d] = unit_rows(cells_ref[block_of(lane, d), :])
    eye = diagonal(BLOCK)
    own = unit_ref[0]
    col_mean = upright(mean_ref[:, block_of(lane, 0)], eye)
    left = with_ones(start_ref[:, block_of(lane, 0)].astype(bf16))
    rows = product_ref.shape[1]
    for d in range(lanes):
        weights = affinity(own, unit_ref[d], col_mean, mean_ref[:, block_of(lane, d)])
        if d == 0:
            weights = jnp.where(eye, 0.0, weights)
        weights = weights.astype(bf16)
        weight_ref[d] = weights
        product_ref[d] = jnp.dot(left, weights, preferred_element_type=f32)[:rows]


def next_kernel(
    lanes,
    columns,
    unit_ref,
    cells_ref,
    side_ref,
    mean_ref,
    start_ref,
    own_ref,
    *rest,
):
    lists, (weight_ref, mask_ref, *product_refs, back_ref) = rest[:lanes], rest[lanes:]
    lane = lax.axis_index("cols")
    group = lax.axis_index("rows")
    blocks = lax.axis_size("rows") * lanes
    size = columns
    listed = jnp.concatenate([ref[...] for ref in lists], axis=0)
    here = [listed[4 * p : 4 * p + 1] * blocks + listed[4 * p + 1 : 4 * p + 2] for p in range(lanes)]
    after = [
        listed[4 * p + 2 : 4 * p + 3] * blocks + listed[4 * p + 3 : 4 * p + 4] for p in range(lanes)
    ]
    here = jnp.concatenate(here, axis=0)
    after = jnp.concatenate(after, axis=0)

    def live(codes, row_block, col_block):
        hit = jnp.where(codes == row_block * blocks + col_block, 1.0, 0.0)
        return jnp.max(jnp.max(hit, axis=1, keepdims=True), axis=0, keepdims=True)

    eye = diagonal(BLOCK)
    col_unit = unit_rows(cells_ref[...])
    col_mean = upright(side_ref[size : size + 1, :].astype(f32), eye)
    left = with_ones(side_ref[:size, :])
    rows = own_ref.shape[1]
    back = jnp.zeros((rows, BLOCK), f32)
    for d in range(lanes):
        row_block = group * lanes + (lane ^ d)
        own_live = live(here, row_block, group * lanes + lane)
        next_live = live(here, row_block, (group + 1) * lanes + lane)
        back_live = live(after, (group + 1) * lanes + lane, row_block)
        for at, value in ((0, own_live), (1, next_live), (2, back_live)):
            mask_ref[at * lanes + d : at * lanes + d + 1, :] = jnp.broadcast_to(
                value, (1, mask_ref.shape[1])
            )
        weights = affinity(col_unit, unit_ref[d], col_mean, mean_ref[:, block_of(lane, d)])
        weights = weights.astype(bf16)
        weight_ref[d] = weights
        product = jnp.dot(left, weights, preferred_element_type=f32)[:rows]
        product_refs[d][...] = own_live * own_ref[d] + next_live * product
        narrow = with_ones(start_ref[:, block_of(lane, d)].astype(bf16))
        back = back + back_live * nt(narrow, weights)[:rows]
    back_ref[...] = back


def smooth_kernel(size, *refs):
    *parts, smooth_ref, degree_ref = refs
    total = parts[0][...]
    for part in parts[1:]:
        total = total + part[...]
    degree = total[size : size + 1]
    smooth_ref[...] = total[:size] / degree
    degree_ref[...] = jnp.broadcast_to(degree, degree_ref.shape)


def sweep_kernel(lanes, total, own_ref, weight_ref, mask_ref, next_ref, *rest):
    blocks, (*product_refs, back_ref, gram_ref) = rest[:lanes], rest[lanes:]
    size = next_ref.shape[0]
    own_left = pieces(blocks[0][...])
    next_left = pieces(next_ref[...])
    back = jnp.zeros((size, BLOCK), f32)

    def mask(at, d):
        return mask_ref[at * lanes + d : at * lanes + d + 1, :]

    for d in range(lanes):
        own = joined(jnp.dot(own_left, own_ref[d], preferred_element_type=f32), size)
        after = joined(jnp.dot(next_left, weight_ref[d], preferred_element_type=f32), size)
        product_refs[d][...] = mask(0, d) * own + mask(1, d) * after
        left = own_left if d == 0 else pieces(blocks[d][...])
        back = back + mask(2, d) * joined(nt(left, weight_ref[d]), size)
    back_ref[...] = back
    gram_ref[...] = gram_of([block[...] for block in blocks], total)


def resmooth_kernel(degree_ref, *refs):
    *parts, smooth_ref = refs
    total = parts[0][...]
    for part in parts[1:]:
        total = total + part[...]
    smooth_ref[...] = total / degree_ref[0:1, :]


def first_solve_kernel(lanes, total, *refs):
    grams, blocks, smooth_ref, gram_ref = refs[: -lanes - 2], refs[-lanes - 2 : -2], refs[-2], refs[-1]
    gram = grams[0][...]
    for part in grams[1:]:
        gram = gram + part[...]
    inverse = inverse_factor(gram)
    solved = []
    for d in range(lanes):
        value = times(inverse, blocks[d][...])
        smooth_ref[d] = value
        solved.append(value)
    gram_ref[...] = gram_of(solved, total)


def last_solve_kernel(lanes, smooth_ref, *refs):
    *grams, out_ref = refs
    lane = lax.axis_index("cols")
    gram = grams[0][...]
    for part in grams[1:]:
        gram = gram + part[...]
    inverse = inverse_factor(gram)
    for d in range(lanes):
        out_ref[:, block_of(lane, d)] = times(inverse, smooth_ref[d])


def call(body, outs, *args):
    return pl.pallas_call(
        body,
        out_shape=[jax.ShapeDtypeStruct(shape, kind) for shape, kind in outs],
        in_specs=[pl.BlockSpec(memory_space=pltpu.VMEM)] * len(args),
        out_specs=[pl.BlockSpec(memory_space=pltpu.VMEM)] * len(outs),
        compiler_params=pltpu.CompilerParams(vmem_limit_bytes=40 * 1024 * 1024),
    )(*args)


def local(embeddings, knn_mean, pair_rows, pair_cols, pair_count, start_block):
    rows_here, width = embeddings.shape
    size = start_block.shape[0]
    slots = pair_rows.shape[2]
    lanes = lax.axis_size("cols")
    lane = lax.axis_index("cols")
    groups = lax.axis_size("rows")
    total = rows_here * groups
    assert rows_here == lanes * BLOCK and lanes & (lanes - 1) == 0 and groups & (groups - 1) == 0
    wide = size + 8

    first = lane * BLOCK
    next_cells = shift(lax.dynamic_slice_in_dim(embeddings, first, BLOCK, 0), -1)
    live = jnp.arange(slots, dtype=jnp.int32) < pair_count[0, 0]
    mine = jnp.stack([jnp.where(live, pair_rows[0, 0], -1), jnp.where(live, pair_cols[0, 0], -1)])
    mine = jnp.pad(mine, ((0, 0), (0, 128 - slots)), constant_values=-1)
    lists = lane_swaps(jnp.concatenate([mine, shift(mine, -1)], axis=0))
    side = jnp.concatenate(
        [
            lax.dynamic_slice_in_dim(start_block, first, BLOCK, 1).astype(bf16),
            jnp.broadcast_to(lax.dynamic_slice_in_dim(knn_mean, first, BLOCK, 0)[None], (16, BLOCK)),
        ],
        axis=0,
    )
    next_side = shift(side, -1)
    mean = knn_mean.astype(f32)[None, :]

    unit, own_weights, own_product = call(
        functools.partial(own_kernel, lanes),
        [
            ((lanes, BLOCK, width), bf16),
            ((lanes, BLOCK, BLOCK), bf16),
            ((lanes, wide, BLOCK), f32),
        ],
        embeddings,
        mean,
        start_block,
    )
    next_weights, masks, *products, back = call(
        functools.partial(next_kernel, lanes, size),
        [((lanes, BLOCK, BLOCK), bf16), ((16, BLOCK), f32)] + [((wide, BLOCK), f32)] * (lanes + 1),
        unit,
        next_cells,
        next_side,
        mean,
        start_block,
        own_product,
        *lists,
    )

    def scattered(products, back):
        came = [swap(products[d], "cols", d) for d in range(1, lanes)]
        return [products[0], *came, shift(back, 1)]

    smooth, degree = call(
        functools.partial(smooth_kernel, size),
        [((size, BLOCK), f32), ((8, BLOCK), f32)],
        *scattered(products, back),
    )

    *products, back, gram = call(
        functools.partial(sweep_kernel, lanes, total),
        [((size, BLOCK), f32)] * (lanes + 1) + [((size, size), f32)],
        own_weights,
        next_weights,
        masks,
        shift(smooth, -1),
        *lane_swaps(smooth),
    )
    (smooth,) = call(resmooth_kernel, [((size, BLOCK), f32)], degree, *scattered(products, back))

    def stages(gram):
        parts = [gram]
        for offsets in row_stages(groups):
            whole = sum(parts[1:], parts[0])
            parts = [whole] + [swap(whole, "rows", offset) for offset in offsets]
        return parts

    smooth, gram = call(
        functools.partial(first_solve_kernel, lanes, total),
        [((lanes, size, BLOCK), f32), ((size, size), f32)],
        *stages(gram),
        *lane_swaps(smooth),
    )
    (vector,) = call(
        functools.partial(last_solve_kernel, lanes),
        [((size, rows_here), f32)],
        smooth,
        *stages(gram),
    )
    return vector


def solution(mesh):
    in_specs = (
        P("rows", None),
        P("rows"),
        P("rows", "cols", None),
        P("rows", "cols", None),
        P("rows", "cols"),
        P(None, "rows"),
    )
    out_specs = P(None, "rows")
    return jax.shard_map(local, mesh=mesh, in_specs=in_specs, out_specs=out_specs, check_vma=False)
```

```python
import functools
import math

import jax
import jax.numpy as jnp
from jax import lax
from jax.experimental import pallas as pl
from jax.experimental.pallas import tpu as pltpu
from jax.sharding import PartitionSpec as P

BLOCK = 256
ONES = 16

sharpness = 10.0
epsilon = 1e-06

HIGHEST = lax.Precision.HIGHEST
f32 = jnp.float32
bf16 = jnp.bfloat16


def shift(cells, step):
    count = lax.axis_size("rows")
    return lax.ppermute(cells, "rows", [(i, (i + step) % count) for i in range(count)])


def swap(cells, axis, offset):
    count = lax.axis_size(axis)
    return lax.ppermute(cells, axis, [(i, i ^ offset) for i in range(count)])


def lane_swaps(cells):
    return [cells] + [swap(cells, "cols", d) for d in range(1, lax.axis_size("cols"))]


def row_stages(count):
    bits = count.bit_length() - 1
    stages = []
    low = 0
    while low < bits:
        wide = 1 if (bits - low) % 2 else 2
        stages.append([m << low for m in range(1, 1 << wide)])
        low += wide
    return stages


def nt(left, right):
    return lax.dot_general(left, right, (((1,), (1,)), ((), ())), preferred_element_type=f32)


def unit_rows(cells):
    values = cells.astype(f32)
    scale = lax.rsqrt(jnp.mean(values * values, axis=1, keepdims=True) + epsilon)
    return (values * (scale * (1.0 / math.sqrt(cells.shape[1])))).astype(bf16)


def diagonal(size):
    return lax.broadcasted_iota(jnp.int32, (size, size), 0) == lax.broadcasted_iota(
        jnp.int32, (size, size), 1
    )


def upright(row, eye):
    return jnp.sum(jnp.where(eye, row, 0.0), axis=1, keepdims=True)


def affinity(col_unit, row_unit, col_mean, row_mean):
    scores = nt(col_unit, row_unit)
    return jnp.exp((2.0 * sharpness) * scores / (col_mean + row_mean))


def with_ones(narrow):
    return jnp.concatenate([narrow, jnp.ones((ONES, narrow.shape[1]), bf16)], axis=0)


def pieces(values):
    first = values.astype(bf16)
    rest = values - first.astype(f32)
    second = rest.astype(bf16)
    third = (rest - second.astype(f32)).astype(bf16)
    return jnp.concatenate([first, second, third], axis=0)


def joined(product, size):
    return product[:size] + (product[size : 2 * size] + product[2 * size :])


def inverse_factor(gram):
    size = gram.shape[0]
    tile = 8
    count = size // tile
    eye = jnp.where(diagonal(size), 1.0, 0.0).astype(f32)
    table = jnp.concatenate([gram, eye], axis=1)
    parts = [table[g * tile : (g + 1) * tile] for g in range(count)]
    shape = (tile, 2 * size)
    place = lax.broadcasted_iota(jnp.int32, shape, 0)

    def spread(piece):
        return jnp.broadcast_to(piece, shape)

    out = []
    for b in range(count):
        first = b * tile
        columns = [
            [spread(parts[g][:, first + t : first + t + 1]) for g in range(b, count)]
            for t in range(tile)
        ]
        home = parts[b]
        scales = jnp.ones(shape, f32)
        for t in range(tile):
            scale = lax.rsqrt(spread(columns[t][0][t : t + 1]))
            scales = jnp.where(place == t, scale, scales)
            factor = [column * scale for column in columns[t]]
            factor[0] = jnp.where(place > t, factor[0], 0.0)
            for u in range(t + 1, tile):
                ahead = spread(columns[u][0][t : t + 1]) * scale
                columns[u] = [c - f * ahead for c, f in zip(columns[u], factor)]
            row = spread(home[t : t + 1]) * scale
            home = home - factor[0] * row
            for g in range(b + 1, count):
                parts[g] = parts[g] - factor[g - b] * row
        out.append((home * scales)[:, size:])
    return jnp.concatenate(out, axis=0)


def times(left, right):
    return jnp.dot(left, right, precision=HIGHEST, preferred_element_type=f32)


def gram_of(blocks, total):
    acc = None
    for block in blocks:
        term = lax.dot_general(
            block, block, (((1,), (1,)), ((), ())), precision=HIGHEST, preferred_element_type=f32
        )
        acc = term if acc is None else acc + term
    return acc * (1.0 / total)


def block_of(lane, d):
    return pl.ds(pl.multiple_of((lane ^ d) * BLOCK, BLOCK), BLOCK)


def prep_kernel(lanes, mean_ref, start_ref, *refs):
    lists, (side_ref, mask_ref) = refs[:lanes], refs[lanes:]
    lane = lax.axis_index("cols")
    group = lax.axis_index("rows")
    blocks = lax.axis_size("rows") * lanes
    size = start_ref.shape[0]
    codes = jnp.concatenate([ref[0:1] * blocks + ref[1:2] for ref in lists], axis=0)

    def live(row_block, col_block):
        hit = jnp.where(codes == row_block * blocks + col_block, 1.0, 0.0)
        hit = jnp.max(jnp.max(hit, axis=1, keepdims=True), axis=0, keepdims=True)
        return jnp.broadcast_to(hit, (1, BLOCK))

    mine = group * lanes + lane
    rows = [group * lanes + (lane ^ d) for d in range(lanes)]
    masks = [live(row, mine) for row in rows] + [live(row, mine + lanes) for row in rows]
    mask_ref[...] = jnp.concatenate(masks, axis=0)
    back = [live(mine, row - lanes) for row in rows]
    means = mean_ref[:, block_of(lane, 0)]
    pad = jnp.zeros((side_ref.shape[0] - size - lanes - 1, BLOCK), f32)
    start = start_ref[:, block_of(lane, 0)]
    side_ref[...] = jnp.concatenate([start, means, *back, pad], axis=0).astype(bf16)


def own_kernel(lanes, cells_ref, mean_ref, start_ref, unit_ref, weight_ref, product_ref):
    lane = lax.axis_index("cols")
    for d in range(lanes):
        unit_ref[d] = unit_rows(cells_ref[block_of(lane, d), :])
    eye = diagonal(BLOCK)
    own = unit_ref[0]
    col_mean = upright(mean_ref[:, block_of(lane, 0)], eye)
    left = with_ones(start_ref[:, block_of(lane, 0)].astype(bf16))
    rows = product_ref.shape[1]
    for d in range(lanes):
        weights = affinity(own, unit_ref[d], col_mean, mean_ref[:, block_of(lane, d)])
        if d == 0:
            weights = jnp.where(eye, 0.0, weights)
        weights = weights.astype(bf16)
        weight_ref[d] = weights
        product_ref[d] = jnp.dot(left, weights, preferred_element_type=f32)[:rows]


def next_kernel(lanes, *refs):
    unit_ref, cells_ref, side_ref, mean_ref, start_ref, own_ref, mask_ref, *outs = refs
    weight_ref, keep_ref, core_ref, back_ref = outs
    lane = lax.axis_index("cols")
    size = start_ref.shape[0]
    col_unit = unit_rows(cells_ref[...])
    after = side_ref[size:, :].astype(f32)
    col_mean = upright(after[0:1], diagonal(BLOCK))
    left = with_ones(side_ref[:size, :])
    rows = own_ref.shape[1]
    back = jnp.zeros((rows, BLOCK), f32)
    for d in range(lanes):
        weights = affinity(col_unit, unit_ref[d], col_mean, mean_ref[:, block_of(lane, d)])
        weights = weights.astype(bf16)
        weight_ref[d] = weights
        product = jnp.dot(left, weights, preferred_element_type=f32)[:rows]
        own = mask_ref[d : d + 1, :] * own_ref[d]
        halves(d, keep_ref, core_ref)[...] = own + mask_ref[lanes + d : lanes + d + 1, :] * product
        narrow = with_ones(start_ref[:, block_of(lane, d)].astype(bf16))
        back = back + after[1 + d : 2 + d] * nt(narrow, weights)[:rows]
    back_ref[...] = back


def halves(d, keep_ref, core_ref):
    return (core_ref if d % 2 else keep_ref).at[d // 2]


def pair_kernel(keep_ref, came_ref, own_ref, *away_refs):
    own_ref[...] = keep_ref[0] + came_ref[0]
    for m, away_ref in enumerate(away_refs):
        away_ref[...] = keep_ref[m + 1] + came_ref[m + 1]


def smooth_kernel(size, *refs):
    *parts, smooth_ref, degree_ref = refs
    total = parts[0][...]
    for part in parts[1:]:
        total = total + part[...]
    degree = total[size : size + 1]
    smooth_ref[...] = total[:size] / degree
    degree_ref[...] = jnp.broadcast_to(degree, degree_ref.shape)


def sweep_kernel(lanes, total, own_ref, weight_ref, mask_ref, side_ref, next_ref, *rest):
    blocks, (keep_ref, core_ref, back_ref, gram_ref) = rest[:lanes], rest[lanes:]
    size = next_ref.shape[0]
    own_left = pieces(blocks[0][...])
    next_left = pieces(next_ref[...])
    back_masks = side_ref[size:, :].astype(f32)
    back = jnp.zeros((size, BLOCK), f32)
    for d in range(lanes):
        own = joined(jnp.dot(own_left, own_ref[d], preferred_element_type=f32), size)
        after = joined(jnp.dot(next_left, weight_ref[d], preferred_element_type=f32), size)
        own = mask_ref[d : d + 1, :] * own
        halves(d, keep_ref, core_ref)[...] = own + mask_ref[lanes + d : lanes + d + 1, :] * after
        left = own_left if d == 0 else pieces(blocks[d][...])
        back = back + back_masks[1 + d : 2 + d] * joined(nt(left, weight_ref[d]), size)
    back_ref[...] = back
    gram_ref[...] = gram_of([block[...] for block in blocks], total)


def resmooth_kernel(degree_ref, *refs):
    *parts, smooth_ref = refs
    total = parts[0][...]
    for part in parts[1:]:
        total = total + part[...]
    smooth_ref[...] = total / degree_ref[0:1, :]


def factor_kernel(*refs):
    *grams, inverse_ref = refs
    gram = grams[0][...]
    for part in grams[1:]:
        gram = gram + part[...]
    inverse_ref[...] = inverse_factor(gram)


def first_solve_kernel(lanes, total, inverse_ref, *refs):
    blocks, (smooth_ref, gram_ref) = refs[:lanes], refs[lanes:]
    inverse = inverse_ref[...]
    solved = []
    for d in range(lanes):
        value = times(inverse, blocks[d][...])
        smooth_ref[d] = value
        solved.append(value)
    gram_ref[...] = gram_of(solved, total)


def last_solve_kernel(lanes, smooth_ref, *refs):
    *grams, out_ref = refs
    lane = lax.axis_index("cols")
    gram = grams[0][...]
    for part in grams[1:]:
        gram = gram + part[...]
    inverse = inverse_factor(gram)
    for d in range(lanes):
        out_ref[:, block_of(lane, d)] = times(inverse, smooth_ref[d])


def call(body, outs, *args):
    return pl.pallas_call(
        body,
        out_shape=[jax.ShapeDtypeStruct(shape, kind) for shape, kind in outs],
        in_specs=[pl.BlockSpec(memory_space=pltpu.VMEM)] * len(args),
        out_specs=[pl.BlockSpec(memory_space=pltpu.VMEM)] * len(outs),
        compiler_params=pltpu.CompilerParams(vmem_limit_bytes=40 * 1024 * 1024),
    )(*args)


def local(embeddings, knn_mean, pair_rows, pair_cols, pair_count, start_block):
    rows_here, width = embeddings.shape
    size = start_block.shape[0]
    slots = pair_rows.shape[2]
    lanes = lax.axis_size("cols")
    lane = lax.axis_index("cols")
    groups = lax.axis_size("rows")
    total = rows_here * groups
    assert rows_here == lanes * BLOCK and lanes & (lanes - 1) == 0 and groups & (groups - 1) == 0
    wide = size + 8

    next_cells = shift(lax.dynamic_slice_in_dim(embeddings, lane * BLOCK, BLOCK, 0), -1)
    live = jnp.arange(slots, dtype=jnp.int32) < pair_count[0, 0]
    mine = jnp.stack([jnp.where(live, pair_rows[0, 0], -1), jnp.where(live, pair_cols[0, 0], -1)])
    mine = jnp.pad(mine, ((0, 0), (0, 128 - slots)), constant_values=-1)
    mean = knn_mean.astype(f32)[None, :]
    side, masks = call(
        functools.partial(prep_kernel, lanes),
        [((size + 16, BLOCK), bf16), ((2 * lanes, BLOCK), f32)],
        mean,
        start_block,
        *lane_swaps(mine),
    )
    next_side = shift(side, -1)
    mean, masks = lax.optimization_barrier((mean, masks))

    unit, own_weights, own_product = call(
        functools.partial(own_kernel, lanes),
        [
            ((lanes, BLOCK, width), bf16),
            ((lanes, BLOCK, BLOCK), bf16),
            ((lanes, wide, BLOCK), f32),
        ],
        embeddings,
        mean,
        start_block,
    )
    next_weights, keep, core, back = call(
        functools.partial(next_kernel, lanes),
        [((lanes, BLOCK, BLOCK), bf16)]
        + [((lanes // 2, wide, BLOCK), f32)] * 2
        + [((wide, BLOCK), f32)],
        unit,
        next_cells,
        next_side,
        mean,
        start_block,
        own_product,
        masks,
    )

    def scattered(keep, core, back):
        back = shift(back, 1)
        rows = keep.shape[1]
        own, *away = call(
            pair_kernel, [((rows, BLOCK), f32)] * (lanes // 2), keep, swap(core, "cols", 1)
        )
        return [own, *(swap(part, "cols", 2 * m + 2) for m, part in enumerate(away)), back]

    smooth, degree = call(
        functools.partial(smooth_kernel, size),
        [((size, BLOCK), f32), ((8, BLOCK), f32)],
        *scattered(keep, core, back),
    )

    keep, core, back, gram = call(
        functools.partial(sweep_kernel, lanes, total),
        [((lanes // 2, size, BLOCK), f32)] * 2 + [((size, BLOCK), f32), ((size, size), f32)],
        own_weights,
        next_weights,
        masks,
        next_side,
        shift(smooth, -1),
        *lane_swaps(smooth),
    )

    def stage(parts, offsets):
        whole = sum(parts[1:], parts[0])
        return [whole] + [swap(whole, "rows", offset) for offset in offsets]

    first, *others = row_stages(groups)
    grams = stage([gram], first)
    products = scattered(keep, core, back)
    if others:
        whole, *products = lax.optimization_barrier((sum(grams[1:], grams[0]), *products))
        grams = [whole] + [swap(whole, "rows", offset) for offset in others[0]]
    (smooth,) = call(resmooth_kernel, [((size, BLOCK), f32)], degree, *products)
    for offsets in others[1:]:
        grams = stage(grams, offsets)
    (inverse,) = call(factor_kernel, [((size, size), f32)], *grams)
    smooth, gram = call(
        functools.partial(first_solve_kernel, lanes, total),
        [((lanes, size, BLOCK), f32), ((size, size), f32)],
        inverse,
        *lane_swaps(smooth),
    )
    grams = [gram]
    for offsets in row_stages(groups):
        grams = stage(grams, offsets)
    (vector,) = call(
        functools.partial(last_solve_kernel, lanes), [((size, rows_here), f32)], smooth, *grams
    )
    return vector


def solution(mesh):
    in_specs = (
        P("rows", None),
        P("rows"),
        P("rows", "cols", None),
        P("rows", "cols", None),
        P("rows", "cols"),
        P(None, "rows"),
    )
    out_specs = P(None, "rows")
    return jax.shard_map(local, mesh=mesh, in_specs=in_specs, out_specs=out_specs, check_vma=False)
```

```python
import functools
import math

import jax
import jax.numpy as jnp
from jax import lax
from jax.experimental import pallas as pl
from jax.experimental.pallas import tpu as pltpu
from jax.sharding import PartitionSpec as P

BLOCK = 256
ONES = 16

sharpness = 10.0
epsilon = 1e-06

HIGHEST = lax.Precision.HIGHEST
f32 = jnp.float32
bf16 = jnp.bfloat16


def shift(cells, step):
    count = lax.axis_size("rows")
    return lax.ppermute(cells, "rows", [(i, (i + step) % count) for i in range(count)])


def swap(cells, axis, offset):
    count = lax.axis_size(axis)
    return lax.ppermute(cells, axis, [(i, i ^ offset) for i in range(count)])


def lane_swaps(cells):
    return [cells] + [swap(cells, "cols", d) for d in range(1, lax.axis_size("cols"))]


def all_rows(cells):
    bits = lax.axis_size("rows").bit_length() - 1
    parts = [cells]
    low = 0
    while low < bits:
        wide = 1 if (bits - low) % 2 else 2
        whole = sum(parts[1:], parts[0])
        parts = [whole] + [swap(whole, "rows", m << low) for m in range(1, 1 << wide)]
        low += wide
    return parts


def shares(cells):
    groups, lanes = lax.axis_size("rows"), lax.axis_size("cols")
    if groups % lanes or groups // lanes > 4:
        return [sum(all_rows(cells)) * (1.0 / lanes)]
    each = groups // lanes
    parts = []
    for part in range(each):
        pairs = [
            (r * lanes + lane, (r ^ (lane * each + part)) * lanes + lane)
            for r in range(groups)
            for lane in range(lanes)
        ]
        parts.append(lax.ppermute(cells, ("rows", "cols"), pairs))
    return parts


def nt(left, right):
    return lax.dot_general(left, right, (((1,), (1,)), ((), ())), preferred_element_type=f32)


def unit_rows(cells):
    values = cells.astype(f32)
    scale = lax.rsqrt(jnp.mean(values * values, axis=1, keepdims=True) + epsilon)
    return (values * (scale * (1.0 / math.sqrt(cells.shape[1])))).astype(bf16)


def diagonal(size):
    return lax.broadcasted_iota(jnp.int32, (size, size), 0) == lax.broadcasted_iota(
        jnp.int32, (size, size), 1
    )


def upright(row, eye):
    return jnp.sum(jnp.where(eye, row, 0.0), axis=1, keepdims=True)


def affinity(col_unit, row_unit, col_mean, row_mean):
    scores = nt(col_unit, row_unit)
    return jnp.exp((2.0 * sharpness) * scores / (col_mean + row_mean))


def with_ones(narrow):
    return jnp.concatenate([narrow, jnp.ones((ONES, narrow.shape[1]), bf16)], axis=0)


def pieces(values):
    first = values.astype(bf16)
    rest = values - first.astype(f32)
    second = rest.astype(bf16)
    third = (rest - second.astype(f32)).astype(bf16)
    return jnp.concatenate([first, second, third], axis=0)


def joined(product, size):
    return product[:size] + (product[size : 2 * size] + product[2 * size :])


def inverse_factor(gram):
    size = gram.shape[0]
    tile = 8
    count = size // tile
    eye = jnp.where(diagonal(size), 1.0, 0.0).astype(f32)
    table = jnp.concatenate([gram, eye], axis=1)
    parts = [table[g * tile : (g + 1) * tile] for g in range(count)]
    shape = (tile, 2 * size)
    place = lax.broadcasted_iota(jnp.int32, shape, 0)

    def spread(piece):
        return jnp.broadcast_to(piece, shape)

    out = []
    for b in range(count):
        first = b * tile
        columns = [
            [spread(parts[g][:, first + t : first + t + 1]) for g in range(b, count)]
            for t in range(tile)
        ]
        home = parts[b]
        scales = jnp.ones(shape, f32)
        for t in range(tile):
            scale = lax.rsqrt(spread(columns[t][0][t : t + 1]))
            scales = jnp.where(place == t, scale, scales)
            factor = [column * scale for column in columns[t]]
            factor[0] = jnp.where(place > t, factor[0], 0.0)
            for u in range(t + 1, tile):
                ahead = spread(columns[u][0][t : t + 1]) * scale
                columns[u] = [c - f * ahead for c, f in zip(columns[u], factor)]
            row = spread(home[t : t + 1]) * scale
            home = home - factor[0] * row
            for g in range(b + 1, count):
                parts[g] = parts[g] - factor[g - b] * row
        out.append((home * scales)[:, size:])
    return jnp.concatenate(out, axis=0)


def times(left, right):
    return jnp.dot(left, right, precision=HIGHEST, preferred_element_type=f32)


def gram_of(blocks, total):
    acc = None
    for block in blocks:
        term = lax.dot_general(
            block, block, (((1,), (1,)), ((), ())), precision=HIGHEST, preferred_element_type=f32
        )
        acc = term if acc is None else acc + term
    return acc * (1.0 / total)


def block_of(lane, d):
    return pl.ds(pl.multiple_of((lane ^ d) * BLOCK, BLOCK), BLOCK)


def prep_kernel(lanes, knn_ref, start_ref, *refs):
    lists, (side_ref, mask_ref, mean_ref, left_ref) = refs[:lanes], refs[lanes:]
    lane = lax.axis_index("cols")
    group = lax.axis_index("rows")
    blocks = lax.axis_size("rows") * lanes
    size = start_ref.shape[0]
    stride = 4 * blocks
    slot = lax.broadcasted_iota(jnp.int32, (1, lists[0].shape[1]), 1)
    codes = [jnp.where(slot < ref[2:3], ref[0:1] * stride + ref[1:2], -stride) for ref in lists]
    codes = jnp.concatenate(codes, axis=0)

    def live(row_block, col_block):
        hit = jnp.where(codes == row_block * stride + col_block, 1.0, 0.0)
        hit = jnp.max(jnp.max(hit, axis=1, keepdims=True), axis=0, keepdims=True)
        return jnp.broadcast_to(hit, (1, BLOCK))

    mine = group * lanes + lane
    rows = [group * lanes + (lane ^ d) for d in range(lanes)]
    masks = [live(row, mine) for row in rows] + [live(row, mine + lanes) for row in rows]
    mask_ref[...] = jnp.concatenate(masks, axis=0)
    back = [live(mine, row - lanes) for row in rows]
    knn = knn_ref[...].astype(f32)
    mean_ref[...] = jnp.concatenate([knn[k : k + 1] for k in range(knn.shape[0])], axis=1)
    means = mean_ref[:, block_of(lane, 0)]
    pad = jnp.zeros((side_ref.shape[0] - size - lanes - 1, BLOCK), f32)
    start = start_ref[:, block_of(lane, 0)]
    side_ref[...] = jnp.concatenate([start, means, *back, pad], axis=0).astype(bf16)
    for d in range(lanes):
        left_ref[d] = with_ones(start_ref[:, block_of(lane, d)].astype(bf16))


def own_kernel(lanes, cells_ref, mean_ref, left_ref, unit_ref, weight_ref, product_ref, held, sems):
    lane = lax.axis_index("cols")
    copies = [
        pltpu.make_async_copy(cells_ref.at[block_of(lane, d), :], held.at[d], sems.at[d])
        for d in range(lanes)
    ]
    for copy in copies:
        copy.start()
    eye = diagonal(BLOCK)
    col_mean = upright(mean_ref[:, block_of(lane, 0)], eye)
    left = left_ref[0]
    rows = product_ref.shape[1]
    for d in range(lanes):
        copies[d].wait()
        unit = unit_rows(held[d])
        unit_ref[d] = unit
        if d == 0:
            own = unit
        weights = affinity(own, unit, col_mean, mean_ref[:, block_of(lane, d)])
        if d == 0:
            weights = jnp.where(eye, 0.0, weights)
        weights = weights.astype(bf16)
        weight_ref[d] = weights
        product_ref[d] = jnp.dot(left, weights, preferred_element_type=f32)[:rows]


def next_kernel(lanes, *refs):
    unit_ref, cells_ref, side_ref, mean_ref, left_ref, own_ref, mask_ref, *outs = refs
    weight_ref, keep_ref, core_ref, back_ref = outs
    lane = lax.axis_index("cols")
    size = left_ref.shape[1] - ONES
    col_unit = unit_rows(cells_ref[...])
    after = side_ref[size:, :].astype(f32)
    col_mean = upright(after[0:1], diagonal(BLOCK))
    left = with_ones(side_ref[:size, :])
    rows = own_ref.shape[1]
    back = jnp.zeros((rows, BLOCK), f32)
    for d in range(lanes):
        weights = affinity(col_unit, unit_ref[d], col_mean, mean_ref[:, block_of(lane, d)])
        weights = weights.astype(bf16)
        weight_ref[d] = weights
        product = jnp.dot(left, weights, preferred_element_type=f32)[:rows]
        own = mask_ref[d : d + 1, :] * own_ref[d]
        halves(d, keep_ref, core_ref)[...] = own + mask_ref[lanes + d : lanes + d + 1, :] * product
        back = back + after[1 + d : 2 + d] * nt(left_ref[d], weights)[:rows]
    back_ref[...] = back


def halves(d, keep_ref, core_ref):
    return (core_ref if d % 2 else keep_ref).at[d // 2]


def pair_kernel(keep_ref, came_ref, own_ref, *away_refs):
    own_ref[...] = keep_ref[0] + came_ref[0]
    for m, away_ref in enumerate(away_refs):
        away_ref[...] = keep_ref[m + 1] + came_ref[m + 1]


def smooth_kernel(size, *refs):
    *parts, smooth_ref, degree_ref = refs
    total = added(parts)
    degree = total[size : size + 1]
    smooth_ref[...] = total[:size] / degree
    degree_ref[...] = jnp.broadcast_to(degree, degree_ref.shape)


def sweep_kernel(lanes, total, own_ref, weight_ref, mask_ref, side_ref, next_ref, *rest):
    blocks, (keep_ref, core_ref, back_ref, gram_ref) = rest[:lanes], rest[lanes:]
    size = next_ref.shape[0]
    own_left = pieces(blocks[0][...])
    next_left = pieces(next_ref[...])
    back_masks = side_ref[size:, :].astype(f32)
    back = jnp.zeros((size, BLOCK), f32)
    for d in range(lanes):
        own = joined(jnp.dot(own_left, own_ref[d], preferred_element_type=f32), size)
        after = joined(jnp.dot(next_left, weight_ref[d], preferred_element_type=f32), size)
        own = mask_ref[d : d + 1, :] * own
        halves(d, keep_ref, core_ref)[...] = own + mask_ref[lanes + d : lanes + d + 1, :] * after
        left = own_left if d == 0 else pieces(blocks[d][...])
        back = back + back_masks[1 + d : 2 + d] * joined(nt(left, weight_ref[d]), size)
    back_ref[...] = back
    gram_ref[...] = gram_of([block[...] for block in blocks], total)


def packed(gram):
    size = gram.shape[0]
    wide = BLOCK // size
    tall = size // wide
    return jnp.concatenate([gram[k * tall : (k + 1) * tall] for k in range(wide)], axis=1)


def unpacked(rows, size):
    return jnp.concatenate(
        [rows[:, k * size : (k + 1) * size] for k in range(BLOCK // size)], axis=0
    )


def added(refs):
    total = refs[0][...]
    for ref in refs[1:]:
        total = total + ref[...]
    return total


def resmooth_kernel(terms, degree_ref, *refs):
    parts, grams, out_ref = refs[:terms], refs[terms:-1], refs[-1]
    out_ref[...] = jnp.concatenate(
        [added(parts) / degree_ref[0:1, :], packed(added(grams))], axis=0
    )


def first_solve_kernel(size, total, *refs):
    *blocks, smooth_ref, gram_ref = refs
    gram = unpacked(blocks[0][size:], size)
    for block in blocks[1:]:
        gram = gram + unpacked(block[size:], size)
    inverse = inverse_factor(gram)
    solved = []
    for d, block in enumerate(blocks):
        value = times(inverse, block[:size])
        smooth_ref[d] = value
        solved.append(value)
    gram_ref[...] = gram_of(solved, total)


def last_solve_kernel(lanes, smooth_ref, *refs):
    *grams, out_ref = refs
    lane = lax.axis_index("cols")
    inverse = inverse_factor(added(grams))
    for d in range(lanes):
        out_ref[:, block_of(lane, d)] = times(inverse, smooth_ref[d])


def call(body, outs, *args, scratch=(), apart=()):
    vmem = pl.BlockSpec(memory_space=pltpu.VMEM)
    where = [pl.BlockSpec(memory_space=pl.ANY) if k in apart else vmem for k in range(len(args))]
    return pl.pallas_call(
        body,
        out_shape=[jax.ShapeDtypeStruct(shape, kind) for shape, kind in outs],
        in_specs=where,
        out_specs=[vmem] * len(outs),
        scratch_shapes=list(scratch),
        compiler_params=pltpu.CompilerParams(vmem_limit_bytes=40 * 1024 * 1024),
    )(*args)


def local(embeddings, knn_mean, pair_rows, pair_cols, pair_count, start_block):
    rows_here, width = embeddings.shape
    size = start_block.shape[0]
    slots = pair_rows.shape[2]
    lanes = lax.axis_size("cols")
    lane = lax.axis_index("cols")
    groups = lax.axis_size("rows")
    total = rows_here * groups
    assert rows_here == lanes * BLOCK and lanes & (lanes - 1) == 0 and groups & (groups - 1) == 0
    wide = size + 8

    next_cells = shift(lax.dynamic_slice_in_dim(embeddings, lane * BLOCK, BLOCK, 0), -1)
    counts = jnp.broadcast_to(pair_count, (1, slots))
    mine = jnp.concatenate([pair_rows[0], pair_cols[0], counts], axis=0)
    side, masks, mean, left = call(
        functools.partial(prep_kernel, lanes),
        [
            ((size + ONES, BLOCK), bf16),
            ((2 * lanes, BLOCK), f32),
            ((1, rows_here), f32),
            ((lanes, size + ONES, BLOCK), bf16),
        ],
        knn_mean.reshape(rows_here // 128, 128),
        start_block,
        *lane_swaps(mine),
    )
    next_side = shift(side, -1)

    unit, own_weights, own_product = call(
        functools.partial(own_kernel, lanes),
        [
            ((lanes, BLOCK, width), bf16),
            ((lanes, BLOCK, BLOCK), bf16),
            ((lanes, wide, BLOCK), f32),
        ],
        embeddings,
        mean,
        left,
        scratch=[pltpu.VMEM((lanes, BLOCK, width), bf16), pltpu.SemaphoreType.DMA((lanes,))],
        apart=(0,),
    )
    next_weights, keep, core, back = call(
        functools.partial(next_kernel, lanes),
        [((lanes, BLOCK, BLOCK), bf16)]
        + [((lanes // 2, wide, BLOCK), f32)] * 2
        + [((wide, BLOCK), f32)],
        unit,
        next_cells,
        next_side,
        mean,
        left,
        own_product,
        masks,
    )

    def scattered(keep, core, back):
        back = shift(back, 1)
        rows = keep.shape[1]
        own, *away = call(
            pair_kernel, [((rows, BLOCK), f32)] * (lanes // 2), keep, swap(core, "cols", 1)
        )
        return [own, *(swap(part, "cols", 2 * m + 2) for m, part in enumerate(away)), back]

    smooth, degree = call(
        functools.partial(smooth_kernel, size),
        [((size, BLOCK), f32), ((8, BLOCK), f32)],
        *scattered(keep, core, back),
    )

    keep, core, back, gram = call(
        functools.partial(sweep_kernel, lanes, total),
        [((lanes // 2, size, BLOCK), f32)] * 2 + [((size, BLOCK), f32), ((size, size), f32)],
        own_weights,
        next_weights,
        masks,
        next_side,
        shift(smooth, -1),
        *lane_swaps(smooth),
    )

    products = scattered(keep, core, back)
    (block,) = call(
        functools.partial(resmooth_kernel, len(products)),
        [((size + size * size // BLOCK, BLOCK), f32)],
        degree,
        *products,
        *shares(gram),
    )
    smooth, gram = call(
        functools.partial(first_solve_kernel, size, total),
        [((lanes, size, BLOCK), f32), ((size, size), f32)],
        *lane_swaps(block),
    )
    (vector,) = call(
        functools.partial(last_solve_kernel, lanes),
        [((size, rows_here), f32)],
        smooth,
        *all_rows(gram),
    )
    return vector


def solution(mesh):
    in_specs = (
        P("rows", None),
        P("rows"),
        P("rows", "cols", None),
        P("rows", "cols", None),
        P("rows", "cols"),
        P(None, "rows"),
    )
    out_specs = P(None, "rows")
    return jax.shard_map(local, mesh=mesh, in_specs=in_specs, out_specs=out_specs, check_vma=False)
```

```python
import functools
import math

import jax
import jax.numpy as jnp
from jax import lax
from jax.experimental import pallas as pl
from jax.experimental.pallas import tpu as pltpu
from jax.sharding import PartitionSpec as P

BLOCK = 256
ONES = 16

sharpness = 10.0
epsilon = 1e-06

HIGHEST = lax.Precision.HIGHEST
f32 = jnp.float32
bf16 = jnp.bfloat16


def shift(cells, step):
    count = lax.axis_size("rows")
    return lax.ppermute(cells, "rows", [(i, (i + step) % count) for i in range(count)])


def swap(cells, axis, offset):
    count = lax.axis_size(axis)
    return lax.ppermute(cells, axis, [(i, i ^ offset) for i in range(count)])


def lane_swaps(cells):
    return [cells] + [swap(cells, "cols", d) for d in range(1, lax.axis_size("cols"))]


def all_rows(cells):
    bits = lax.axis_size("rows").bit_length() - 1
    parts = [cells]
    low = 0
    while low < bits:
        wide = 1 if (bits - low) % 2 else 2
        whole = sum(parts[1:], parts[0])
        parts = [whole] + [swap(whole, "rows", m << low) for m in range(1, 1 << wide)]
        low += wide
    return parts


def nt(left, right):
    return lax.dot_general(left, right, (((1,), (1,)), ((), ())), preferred_element_type=f32)


def unit_rows(cells):
    values = cells.astype(f32)
    scale = lax.rsqrt(jnp.mean(values * values, axis=1, keepdims=True) + epsilon)
    return (values * (scale * (1.0 / math.sqrt(cells.shape[1])))).astype(bf16)


def diagonal(size):
    return lax.broadcasted_iota(jnp.int32, (size, size), 0) == lax.broadcasted_iota(
        jnp.int32, (size, size), 1
    )


def upright(row, eye):
    return jnp.sum(jnp.where(eye, row, 0.0), axis=1, keepdims=True)


def affinity(col_unit, row_unit, col_mean, row_mean):
    scores = nt(col_unit, row_unit)
    return jnp.exp((2.0 * sharpness) * scores / (col_mean + row_mean))


def with_ones(narrow):
    return jnp.concatenate([narrow, jnp.ones((ONES, narrow.shape[1]), bf16)], axis=0)


def pieces(values):
    first = values.astype(bf16)
    rest = values - first.astype(f32)
    second = rest.astype(bf16)
    third = (rest - second.astype(f32)).astype(bf16)
    return jnp.concatenate([first, second, third], axis=0)


def joined(product, size):
    return product[:size] + (product[size : 2 * size] + product[2 * size :])


def inverse_factor(gram):
    size = gram.shape[0]
    tile = 8
    count = size // tile
    eye = jnp.where(diagonal(size), 1.0, 0.0).astype(f32)
    table = jnp.concatenate([gram, eye], axis=1)
    parts = [table[g * tile : (g + 1) * tile] for g in range(count)]
    shape = (tile, 2 * size)
    place = lax.broadcasted_iota(jnp.int32, shape, 0)

    def spread(piece):
        return jnp.broadcast_to(piece, shape)

    out = []
    for b in range(count):
        first = b * tile
        columns = [
            [spread(parts[g][:, first + t : first + t + 1]) for g in range(b, count)]
            for t in range(tile)
        ]
        home = parts[b]
        scales = jnp.ones(shape, f32)
        for t in range(tile):
            scale = lax.rsqrt(spread(columns[t][0][t : t + 1]))
            scales = jnp.where(place == t, scale, scales)
            factor = [column * scale for column in columns[t]]
            factor[0] = jnp.where(place > t, factor[0], 0.0)
            for u in range(t + 1, tile):
                ahead = spread(columns[u][0][t : t + 1]) * scale
                columns[u] = [c - f * ahead for c, f in zip(columns[u], factor)]
            row = spread(home[t : t + 1]) * scale
            home = home - factor[0] * row
            for g in range(b + 1, count):
                parts[g] = parts[g] - factor[g - b] * row
        out.append((home * scales)[:, size:])
    return jnp.concatenate(out, axis=0)


def times(left, right):
    return jnp.dot(left, right, precision=HIGHEST, preferred_element_type=f32)


def gram_of(blocks, total):
    acc = None
    for block in blocks:
        term = lax.dot_general(
            block, block, (((1,), (1,)), ((), ())), precision=HIGHEST, preferred_element_type=f32
        )
        acc = term if acc is None else acc + term
    return acc * (1.0 / total)


def block_of(lane, d):
    return pl.ds(pl.multiple_of((lane ^ d) * BLOCK, BLOCK), BLOCK)


def vector_kernel(lanes, knn_ref, start_ref, mean_ref, left_ref):
    lane = lax.axis_index("cols")
    knn = knn_ref[...].astype(f32)
    mean_ref[...] = jnp.concatenate([knn[k : k + 1] for k in range(knn.shape[0])], axis=1)
    for d in range(lanes):
        left_ref[d] = with_ones(start_ref[:, block_of(lane, d)].astype(bf16))


def prep_kernel(lanes, mean_ref, left_ref, *refs):
    lists, (side_ref, mask_ref) = refs[:lanes], refs[lanes:]
    lane = lax.axis_index("cols")
    group = lax.axis_index("rows")
    blocks = lax.axis_size("rows") * lanes
    size = left_ref.shape[1] - ONES
    stride = 4 * blocks
    slot = lax.broadcasted_iota(jnp.int32, (1, lists[0].shape[1]), 1)
    codes = [
        jnp.where(slot < ref[2:3, 0:1], ref[0:1] * stride + ref[1:2], -stride) for ref in lists
    ]
    codes = jnp.concatenate(codes, axis=0)

    def live(row_block, col_block):
        hit = jnp.where(codes == row_block * stride + col_block, 1.0, 0.0)
        hit = jnp.max(jnp.max(hit, axis=1, keepdims=True), axis=0, keepdims=True)
        return jnp.broadcast_to(hit, (1, BLOCK))

    mine = group * lanes + lane
    rows = [group * lanes + (lane ^ d) for d in range(lanes)]
    masks = [live(row, mine) for row in rows] + [live(row, mine + lanes) for row in rows]
    mask_ref[...] = jnp.concatenate(masks, axis=0)
    back = [live(mine, row - lanes) for row in rows]
    means = mean_ref[:, block_of(lane, 0)]
    pad = jnp.zeros((ONES - lanes - 1, BLOCK), f32)
    after = jnp.concatenate([means, *back, pad], axis=0).astype(bf16)
    side_ref[...] = jnp.concatenate([left_ref[0, :size, :], after], axis=0)


def own_kernel(lanes, cells_ref, mean_ref, left_ref, unit_ref, weight_ref, product_ref, held, sems):
    lane = lax.axis_index("cols")
    copies = [
        pltpu.make_async_copy(cells_ref.at[block_of(lane, d), :], held.at[d], sems.at[d])
        for d in range(lanes)
    ]
    for copy in copies:
        copy.start()
    eye = diagonal(BLOCK)
    col_mean = upright(mean_ref[:, block_of(lane, 0)], eye)
    left = left_ref[0]
    rows = product_ref.shape[1]
    for d in range(lanes):
        copies[d].wait()
        unit = unit_rows(held[d])
        unit_ref[d] = unit
        if d == 0:
            own = unit
        weights = affinity(own, unit, col_mean, mean_ref[:, block_of(lane, d)])
        if d == 0:
            weights = jnp.where(eye, 0.0, weights)
        weights = weights.astype(bf16)
        weight_ref[d] = weights
        product_ref[d] = jnp.dot(left, weights, preferred_element_type=f32)[:rows]


def next_kernel(lanes, *refs):
    unit_ref, cells_ref, side_ref, mean_ref, left_ref, own_ref, mask_ref, *outs = refs
    weight_ref, keep_ref, core_ref, back_ref = outs
    lane = lax.axis_index("cols")
    size = left_ref.shape[1] - ONES
    col_unit = unit_rows(cells_ref[...])
    after = side_ref[size:, :].astype(f32)
    col_mean = upright(after[0:1], diagonal(BLOCK))
    left = with_ones(side_ref[:size, :])
    rows = own_ref.shape[1]
    back = jnp.zeros((rows, BLOCK), f32)
    for d in range(lanes):
        weights = affinity(col_unit, unit_ref[d], col_mean, mean_ref[:, block_of(lane, d)])
        weights = weights.astype(bf16)
        weight_ref[d] = weights
        product = jnp.dot(left, weights, preferred_element_type=f32)[:rows]
        own = mask_ref[d : d + 1, :] * own_ref[d]
        halves(d, keep_ref, core_ref)[...] = own + mask_ref[lanes + d : lanes + d + 1, :] * product
        back = back + after[1 + d : 2 + d] * nt(left_ref[d], weights)[:rows]
    back_ref[...] = back


def halves(d, keep_ref, core_ref):
    return (core_ref if d % 2 else keep_ref).at[d // 2]


def pair_kernel(keep_ref, came_ref, own_ref, *away_refs):
    own_ref[...] = keep_ref[0] + came_ref[0]
    for m, away_ref in enumerate(away_refs):
        away_ref[...] = keep_ref[m + 1] + came_ref[m + 1]


def smooth_kernel(size, *refs):
    *parts, smooth_ref, degree_ref = refs
    total = added(parts)
    degree = total[size : size + 1]
    smooth_ref[...] = total[:size] / degree
    degree_ref[...] = jnp.broadcast_to(degree, degree_ref.shape)


def sweep_kernel(lanes, total, own_ref, weight_ref, mask_ref, side_ref, next_ref, *rest):
    blocks, (keep_ref, core_ref, back_ref, gram_ref) = rest[:lanes], rest[lanes:]
    size = next_ref.shape[0]
    own_left = pieces(blocks[0][...])
    next_left = pieces(next_ref[...])
    back_masks = side_ref[size:, :].astype(f32)
    back = jnp.zeros((size, BLOCK), f32)
    for d in range(lanes):
        own = joined(jnp.dot(own_left, own_ref[d], preferred_element_type=f32), size)
        after = joined(jnp.dot(next_left, weight_ref[d], preferred_element_type=f32), size)
        own = mask_ref[d : d + 1, :] * own
        halves(d, keep_ref, core_ref)[...] = own + mask_ref[lanes + d : lanes + d + 1, :] * after
        left = own_left if d == 0 else pieces(blocks[d][...])
        back = back + back_masks[1 + d : 2 + d] * joined(nt(left, weight_ref[d]), size)
    back_ref[...] = back
    gram_ref[...] = gram_of([block[...] for block in blocks], total)


def added(refs):
    total = refs[0][...]
    for ref in refs[1:]:
        total = total + ref[...]
    return total


def resmooth_kernel(degree_ref, *refs):
    *parts, smooth_ref = refs
    smooth_ref[...] = added(parts) / degree_ref[0:1, :]


def grams_kernel(total, first_ref, *refs):
    *blocks, grams_ref = refs
    second = gram_of([block[...] for block in blocks], total)
    grams_ref[...] = jnp.concatenate([first_ref[...], second], axis=1)


def solve_kernel(lanes, *refs):
    blocks, grams, out_ref = refs[:lanes], refs[lanes:-1], refs[-1]
    lane = lax.axis_index("cols")
    size = out_ref.shape[0]
    both = added(grams)
    first = inverse_factor(both[:, :size])
    solved = [times(first, block[...]) for block in blocks]
    half = times(first, both[:, size:])
    gram = lax.dot_general(
        half, first, (((1,), (1,)), ((), ())), precision=HIGHEST, preferred_element_type=f32
    )
    second = inverse_factor(gram)
    for d in range(lanes):
        out_ref[:, block_of(lane, d)] = times(second, solved[d])


def call(body, outs, *args, scratch=(), apart=()):
    vmem = pl.BlockSpec(memory_space=pltpu.VMEM)
    where = [pl.BlockSpec(memory_space=pltpu.HBM) if k in apart else vmem for k in range(len(args))]
    return pl.pallas_call(
        body,
        out_shape=[jax.ShapeDtypeStruct(shape, kind) for shape, kind in outs],
        in_specs=where,
        out_specs=[vmem] * len(outs),
        scratch_shapes=list(scratch),
        compiler_params=pltpu.CompilerParams(vmem_limit_bytes=40 * 1024 * 1024),
    )(*args)


def local(embeddings, knn_mean, pair_rows, pair_cols, pair_count, start_block):
    rows_here, width = embeddings.shape
    size = start_block.shape[0]
    slots = pair_rows.shape[2]
    lanes = lax.axis_size("cols")
    lane = lax.axis_index("cols")
    groups = lax.axis_size("rows")
    total = rows_here * groups
    assert rows_here == lanes * BLOCK and lanes & (lanes - 1) == 0 and groups & (groups - 1) == 0
    wide = size + 8

    next_cells = shift(lax.dynamic_slice_in_dim(embeddings, lane * BLOCK, BLOCK, 0), -1)
    counts = jnp.pad(pair_count, ((0, 0), (0, slots - 1)))
    mine = jnp.concatenate([pair_rows[0], pair_cols[0], counts], axis=0)
    mean, left = call(
        functools.partial(vector_kernel, lanes),
        [((1, rows_here), f32), ((lanes, size + ONES, BLOCK), bf16)],
        knn_mean.reshape(rows_here // 128, 128),
        start_block,
    )
    side, masks = call(
        functools.partial(prep_kernel, lanes),
        [((size + ONES, BLOCK), bf16), ((2 * lanes, BLOCK), f32)],
        mean,
        left,
        *lane_swaps(mine),
    )
    next_side = shift(side, -1)

    unit, own_weights, own_product = call(
        functools.partial(own_kernel, lanes),
        [
            ((lanes, BLOCK, width), bf16),
            ((lanes, BLOCK, BLOCK), bf16),
            ((lanes, wide, BLOCK), f32),
        ],
        embeddings,
        mean,
        left,
        scratch=[pltpu.VMEM((lanes, BLOCK, width), bf16), pltpu.SemaphoreType.DMA((lanes,))],
        apart=(0,),
    )
    next_weights, keep, core, back = call(
        functools.partial(next_kernel, lanes),
        [((lanes, BLOCK, BLOCK), bf16)]
        + [((lanes // 2, wide, BLOCK), f32)] * 2
        + [((wide, BLOCK), f32)],
        unit,
        next_cells,
        next_side,
        mean,
        left,
        own_product,
        masks,
    )

    def scattered(keep, core, back):
        back = shift(back, 1)
        rows = keep.shape[1]
        own, *away = call(
            pair_kernel, [((rows, BLOCK), f32)] * (lanes // 2), keep, swap(core, "cols", 1)
        )
        return [own, *(swap(part, "cols", 2 * m + 2) for m, part in enumerate(away)), back]

    smooth, degree = call(
        functools.partial(smooth_kernel, size),
        [((size, BLOCK), f32), ((8, BLOCK), f32)],
        *scattered(keep, core, back),
    )

    keep, core, back, gram = call(
        functools.partial(sweep_kernel, lanes, total),
        [((lanes // 2, size, BLOCK), f32)] * 2 + [((size, BLOCK), f32), ((size, size), f32)],
        own_weights,
        next_weights,
        masks,
        next_side,
        shift(smooth, -1),
        *lane_swaps(smooth),
    )

    products = scattered(keep, core, back)
    (smooth,) = call(resmooth_kernel, [((size, BLOCK), f32)], degree, *products)
    blocks = lane_swaps(smooth)
    (grams,) = call(
        functools.partial(grams_kernel, total), [((size, 2 * size), f32)], gram, *blocks
    )
    (vector,) = call(
        functools.partial(solve_kernel, lanes),
        [((size, rows_here), f32)],
        *blocks,
        *all_rows(grams),
    )
    return vector


def solution(mesh):
    in_specs = (
        P("rows", None),
        P("rows"),
        P("rows", "cols", None),
        P("rows", "cols", None),
        P("rows", "cols"),
        P(None, "rows"),
    )
    out_specs = P(None, "rows")
    return jax.shard_map(local, mesh=mesh, in_specs=in_specs, out_specs=out_specs, check_vma=False)
```

```python
import functools
import math

import jax
import jax.numpy as jnp
from jax import lax
from jax.experimental import pallas as pl
from jax.experimental.pallas import tpu as pltpu
from jax.sharding import PartitionSpec as P

BLOCK = 256
ONES = 16

sharpness = 10.0
epsilon = 1e-06

HIGHEST = lax.Precision.HIGHEST
f32 = jnp.float32
bf16 = jnp.bfloat16


def shift(cells, step, around=True):
    count = lax.axis_size("rows")
    pairs = [(i, (i + step) % count) for i in range(count) if around or 0 <= i + step < count]
    return lax.ppermute(cells, "rows", pairs)


def swap(cells, axis, offset):
    count = lax.axis_size(axis)
    return lax.ppermute(cells, axis, [(i, i ^ offset) for i in range(count)])


def lane_swaps(cells):
    return [cells] + [swap(cells, "cols", d) for d in range(1, lax.axis_size("cols"))]


def lane_gather(cells):
    lanes = lax.axis_size("cols")
    even = [cells] + [swap(cells, "cols", d) for d in range(2, lanes, 2)]
    odd = [swap(part, "cols", 1) for part in even]
    return [part for pair in zip(even, odd) for part in pair]


def all_rows(cells):
    bits = lax.axis_size("rows").bit_length() - 1
    parts = [cells]
    low = 0
    while low < bits:
        wide = 1 if (bits - low) % 2 else 2
        whole = sum(parts[1:], parts[0])
        parts = [whole] + [swap(whole, "rows", m << low) for m in range(1, 1 << wide)]
        low += wide
    return parts


def nt(left, right):
    return lax.dot_general(left, right, (((1,), (1,)), ((), ())), preferred_element_type=f32)


def unit_rows(cells):
    values = cells.astype(f32)
    scale = lax.rsqrt(jnp.mean(values * values, axis=1, keepdims=True) + epsilon)
    return (values * (scale * (1.0 / math.sqrt(cells.shape[1])))).astype(bf16)


def diagonal(size):
    return lax.broadcasted_iota(jnp.int32, (size, size), 0) == lax.broadcasted_iota(
        jnp.int32, (size, size), 1
    )


def upright(row, eye):
    return jnp.sum(jnp.where(eye, row, 0.0), axis=1, keepdims=True)


def affinity(col_unit, row_unit, col_mean, row_mean):
    scores = nt(col_unit, row_unit)
    return jnp.exp((2.0 * sharpness) * scores / (col_mean + row_mean))


def with_ones(narrow):
    return jnp.concatenate([narrow, jnp.ones((ONES, narrow.shape[1]), bf16)], axis=0)


def pieces(values):
    first = values.astype(bf16)
    rest = values - first.astype(f32)
    second = rest.astype(bf16)
    third = (rest - second.astype(f32)).astype(bf16)
    return jnp.concatenate([first, second, third], axis=0)


def joined(product, size):
    return product[:size] + (product[size : 2 * size] + product[2 * size :])


def inverse_factor(gram):
    size = gram.shape[0]
    tile = 8
    count = size // tile
    eye = jnp.where(diagonal(size), 1.0, 0.0).astype(f32)
    table = jnp.concatenate([gram, eye], axis=1)
    parts = [table[g * tile : (g + 1) * tile] for g in range(count)]
    shape = (tile, 2 * size)
    place = lax.broadcasted_iota(jnp.int32, shape, 0)

    def wide(piece):
        return jnp.broadcast_to(piece, shape)

    def spread(b):
        if b >= count:
            return []
        return [
            {g: wide(parts[g][:, b * tile + t : b * tile + t + 1]) for g in range(b, count)}
            for t in range(tile)
        ]

    scales = [jnp.ones(shape, f32) for _ in range(count)]
    columns = spread(0) + spread(1)
    for b in range(count):
        for t in range(tile):
            scale = lax.rsqrt(wide(columns[t][b][t : t + 1]))
            scales[b] = jnp.where(place == t, scale, scales[b])
            factor = {g: column * scale for g, column in columns[t].items()}
            for u in range(t + 1, len(columns)):
                ahead = wide(columns[t][b + u // tile][u % tile : u % tile + 1]) * scale
                columns[u] = {g: c - factor[g] * ahead for g, c in columns[u].items()}
            factor[b] = jnp.where(place > t, factor[b], 0.0)
            row = wide(parts[b][t : t + 1]) * scale
            for g in range(b, count):
                parts[g] = parts[g] - factor[g] * row
        columns = columns[tile:] + spread(b + 2)
    return jnp.concatenate([(p * s)[:, size:] for p, s in zip(parts, scales)], axis=0)


def times(left, right):
    return jnp.dot(left, right, precision=HIGHEST, preferred_element_type=f32)


def gram_of(blocks, total):
    acc = None
    for block in blocks:
        term = lax.dot_general(
            block, block, (((1,), (1,)), ((), ())), precision=HIGHEST, preferred_element_type=f32
        )
        acc = term if acc is None else acc + term
    return acc * (1.0 / total)


def block_of(lane, d):
    return pl.ds(pl.multiple_of((lane ^ d) * BLOCK, BLOCK), BLOCK)


def vector_kernel(lanes, knn_ref, start_ref, mean_ref, left_ref):
    lane = lax.axis_index("cols")
    knn = knn_ref[...].astype(f32)
    mean_ref[...] = jnp.concatenate([knn[k : k + 1] for k in range(knn.shape[0])], axis=1)
    for d in range(lanes):
        left_ref[d] = with_ones(start_ref[:, block_of(lane, d)].astype(bf16))


def prep_kernel(lanes, mean_ref, left_ref, *refs):
    lists, (side_ref, mask_ref) = refs[:lanes], refs[lanes:]
    lane = lax.axis_index("cols")
    group = lax.axis_index("rows")
    blocks = lax.axis_size("rows") * lanes
    size = left_ref.shape[1] - ONES
    stride = 4 * blocks
    slot = lax.broadcasted_iota(jnp.int32, (1, lists[0].shape[1]), 1)
    codes = [
        jnp.where(slot < ref[2:3, 0:1], ref[0:1] * stride + ref[1:2], -stride) for ref in lists
    ]
    codes = jnp.concatenate(codes, axis=0)

    def live(row_block, col_block):
        hit = jnp.where(codes == row_block * stride + col_block, 1.0, 0.0)
        hit = jnp.max(jnp.max(hit, axis=1, keepdims=True), axis=0, keepdims=True)
        return jnp.broadcast_to(hit, (1, BLOCK))

    mine = group * lanes + lane
    rows = [group * lanes + (lane ^ d) for d in range(lanes)]
    masks = [live(row, mine) for row in rows] + [live(row, mine + lanes) for row in rows]
    mask_ref[...] = jnp.concatenate(masks, axis=0)
    back = [live(mine, row - lanes) for row in rows]
    means = mean_ref[:, block_of(lane, 0)]
    pad = jnp.zeros((ONES - lanes - 1, BLOCK), f32)
    after = jnp.concatenate([means, *back, pad], axis=0).astype(bf16)
    side_ref[...] = jnp.concatenate([left_ref[0, :size, :], after], axis=0)


def own_kernel(lanes, cells_ref, mean_ref, left_ref, unit_ref, weight_ref, product_ref):
    lane = lax.axis_index("cols")
    eye = diagonal(BLOCK)
    col_mean = upright(mean_ref[:, block_of(lane, 0)], eye)
    left = left_ref[0]
    rows = product_ref.shape[1]
    for d in range(lanes):
        unit = unit_rows(cells_ref[block_of(lane, d), :])
        unit_ref[d] = unit
        if d == 0:
            own = unit
        weights = affinity(own, unit, col_mean, mean_ref[:, block_of(lane, d)])
        if d == 0:
            weights = jnp.where(eye, 0.0, weights)
        weights = weights.astype(bf16)
        weight_ref[d] = weights
        product_ref[d] = jnp.dot(left, weights, preferred_element_type=f32)[:rows]


def next_kernel(lanes, *refs):
    unit_ref, cells_ref, side_ref, mean_ref, left_ref, own_ref, mask_ref, *outs = refs
    weight_ref, keep_ref, core_ref, back_ref = outs
    lane = lax.axis_index("cols")
    size = left_ref.shape[1] - ONES
    col_unit = unit_rows(cells_ref[...])
    after = side_ref[size:, :].astype(f32)
    col_mean = upright(after[0:1], diagonal(BLOCK))
    left = with_ones(side_ref[:size, :])
    rows = own_ref.shape[1]
    back = jnp.zeros((rows, BLOCK), f32)
    for d in range(lanes):
        weights = affinity(col_unit, unit_ref[d], col_mean, mean_ref[:, block_of(lane, d)])
        weights = weights.astype(bf16)
        weight_ref[d] = weights
        product = jnp.dot(left, weights, preferred_element_type=f32)[:rows]
        own = mask_ref[d : d + 1, :] * own_ref[d]
        halves(d, keep_ref, core_ref)[...] = own + mask_ref[lanes + d : lanes + d + 1, :] * product
        back = back + after[1 + d : 2 + d] * nt(left_ref[d], weights)[:rows]
    back_ref[...] = back


def halves(d, keep_ref, core_ref):
    return (core_ref if d % 2 else keep_ref).at[d // 2]


def pair_kernel(keep_ref, came_ref, own_ref, *away_refs):
    own_ref[...] = keep_ref[0] + came_ref[0]
    for m, away_ref in enumerate(away_refs):
        away_ref[...] = keep_ref[m + 1] + came_ref[m + 1]


def smooth_kernel(size, *refs):
    *parts, smooth_ref, degree_ref = refs
    total = added(parts)
    degree = total[size : size + 1]
    smooth_ref[...] = total[:size] / degree
    degree_ref[...] = jnp.broadcast_to(degree, degree_ref.shape)


def sweep_kernel(lanes, total, own_ref, weight_ref, mask_ref, side_ref, next_ref, *rest):
    blocks, (keep_ref, core_ref, back_ref, gram_ref) = rest[:lanes], rest[lanes:]
    size = next_ref.shape[0]
    own_left = pieces(blocks[0][...])
    next_left = pieces(next_ref[...])
    back_masks = side_ref[size:, :].astype(f32)
    back = jnp.zeros((size, BLOCK), f32)
    for d in range(lanes):
        own = joined(jnp.dot(own_left, own_ref[d], preferred_element_type=f32), size)
        after = joined(jnp.dot(next_left, weight_ref[d], preferred_element_type=f32), size)
        own = mask_ref[d : d + 1, :] * own
        halves(d, keep_ref, core_ref)[...] = own + mask_ref[lanes + d : lanes + d + 1, :] * after
        left = own_left if d == 0 else pieces(blocks[d][...])
        back = back + back_masks[1 + d : 2 + d] * joined(nt(left, weight_ref[d]), size)
    back_ref[...] = back
    gram_ref[...] = gram_of([block[...] for block in blocks], total)


def added(refs):
    total = refs[0][...]
    for ref in refs[1:]:
        total = total + ref[...]
    return total


def resmooth_kernel(degree_ref, *refs):
    *parts, smooth_ref = refs
    smooth_ref[...] = added(parts) / degree_ref[0:1, :]


def grams_kernel(total, first_ref, *refs):
    *blocks, grams_ref = refs
    second = gram_of([block[...] for block in blocks], total)
    grams_ref[...] = jnp.concatenate([first_ref[...], second], axis=1)


def solve_kernel(lanes, *refs):
    blocks, grams, out_ref = refs[:lanes], refs[lanes:-1], refs[-1]
    lane = lax.axis_index("cols")
    size = out_ref.shape[0]
    both = added(grams)
    first = inverse_factor(both[:, :size])
    solved = [times(first, block[...]) for block in blocks]
    half = times(first, both[:, size:])
    gram = lax.dot_general(
        half, first, (((1,), (1,)), ((), ())), precision=HIGHEST, preferred_element_type=f32
    )
    second = inverse_factor(gram)
    for d in range(lanes):
        out_ref[:, block_of(lane, d)] = times(second, solved[d])


def call(body, outs, *args):
    vmem = pl.BlockSpec(memory_space=pltpu.VMEM)
    return pl.pallas_call(
        body,
        out_shape=[jax.ShapeDtypeStruct(shape, kind) for shape, kind in outs],
        in_specs=[vmem] * len(args),
        out_specs=[vmem] * len(outs),
        compiler_params=pltpu.CompilerParams(vmem_limit_bytes=40 * 1024 * 1024),
    )(*args)


def local(embeddings, knn_mean, pair_rows, pair_cols, pair_count, start_block):
    rows_here, width = embeddings.shape
    size = start_block.shape[0]
    slots = pair_rows.shape[2]
    lanes = lax.axis_size("cols")
    lane = lax.axis_index("cols")
    groups = lax.axis_size("rows")
    total = rows_here * groups
    assert rows_here == lanes * BLOCK and lanes & (lanes - 1) == 0 and groups & (groups - 1) == 0
    wide = size + 8

    next_cells = shift(lax.dynamic_slice_in_dim(embeddings, lane * BLOCK, BLOCK, 0), -1, around=False)
    counts = jnp.pad(pair_count, ((0, 0), (0, slots - 1)))
    mine = jnp.concatenate([pair_rows[0], pair_cols[0], counts], axis=0)
    mean, left = call(
        functools.partial(vector_kernel, lanes),
        [((1, rows_here), f32), ((lanes, size + ONES, BLOCK), bf16)],
        knn_mean.reshape(rows_here // 128, 128),
        start_block,
    )
    side, masks = call(
        functools.partial(prep_kernel, lanes),
        [((size + ONES, BLOCK), bf16), ((2 * lanes, BLOCK), f32)],
        mean,
        left,
        *lane_swaps(mine),
    )
    next_side = shift(side, -1)

    unit, own_weights, own_product = call(
        functools.partial(own_kernel, lanes),
        [
            ((lanes, BLOCK, width), bf16),
            ((lanes, BLOCK, BLOCK), bf16),
            ((lanes, wide, BLOCK), f32),
        ],
        embeddings,
        mean,
        left,
    )
    next_weights, keep, core, back = call(
        functools.partial(next_kernel, lanes),
        [((lanes, BLOCK, BLOCK), bf16)]
        + [((lanes // 2, wide, BLOCK), f32)] * 2
        + [((wide, BLOCK), f32)],
        unit,
        next_cells,
        next_side,
        mean,
        left,
        own_product,
        masks,
    )

    def scattered(keep, core, back):
        back = shift(back, 1)
        rows = keep.shape[1]
        own, *away = call(
            pair_kernel, [((rows, BLOCK), f32)] * (lanes // 2), keep, swap(core, "cols", 1)
        )
        return [own, *(swap(part, "cols", 2 * m + 2) for m, part in enumerate(away)), back]

    smooth, degree = call(
        functools.partial(smooth_kernel, size),
        [((size, BLOCK), f32), ((8, BLOCK), f32)],
        *scattered(keep, core, back),
    )

    keep, core, back, gram = call(
        functools.partial(sweep_kernel, lanes, total),
        [((lanes // 2, size, BLOCK), f32)] * 2 + [((size, BLOCK), f32), ((size, size), f32)],
        own_weights,
        next_weights,
        masks,
        next_side,
        shift(smooth, -1),
        *lane_gather(smooth),
    )

    products = scattered(keep, core, back)
    (smooth,) = call(resmooth_kernel, [((size, BLOCK), f32)], degree, *products)
    blocks = lane_gather(smooth)
    (grams,) = call(
        functools.partial(grams_kernel, total), [((size, 2 * size), f32)], gram, *blocks
    )
    (vector,) = call(
        functools.partial(solve_kernel, lanes),
        [((size, rows_here), f32)],
        *blocks,
        *all_rows(grams),
    )
    return vector


def solution(mesh):
    in_specs = (
        P("rows", None),
        P("rows"),
        P("rows", "cols", None),
        P("rows", "cols", None),
        P("rows", "cols"),
        P(None, "rows"),
    )
    out_specs = P(None, "rows")
    return jax.shard_map(local, mesh=mesh, in_specs=in_specs, out_specs=out_specs, check_vma=False)
```

```python
import functools
import math

import jax
import jax.numpy as jnp
from jax import lax
from jax.experimental import pallas as pl
from jax.experimental.pallas import tpu as pltpu
from jax.sharding import PartitionSpec as P

BLOCK = 256
ONES = 16

sharpness = 10.0
epsilon = 1e-06

HIGHEST = lax.Precision.HIGHEST
f32 = jnp.float32
bf16 = jnp.bfloat16


def shift(cells, step, around=True):
    count = lax.axis_size("rows")
    pairs = [(i, (i + step) % count) for i in range(count) if around or 0 <= i + step < count]
    return lax.ppermute(cells, "rows", pairs)


def swap(cells, axis, offset):
    count = lax.axis_size(axis)
    return lax.ppermute(cells, axis, [(i, i ^ offset) for i in range(count)])


def lane_swaps(cells):
    return [cells] + [swap(cells, "cols", d) for d in range(1, lax.axis_size("cols"))]


def all_rows(cells):
    bits = lax.axis_size("rows").bit_length() - 1
    parts = [cells]
    low = 0
    while low < bits:
        wide = 1 if (bits - low) % 2 else 2
        whole = sum(parts[1:], parts[0])
        parts = [whole] + [swap(whole, "rows", m << low) for m in range((1 << wide) - 1, 0, -1)]
        low += wide
    return parts


def nt(left, right):
    return lax.dot_general(left, right, (((1,), (1,)), ((), ())), preferred_element_type=f32)


def unit_rows(cells):
    values = cells.astype(f32)
    scale = lax.rsqrt(jnp.mean(values * values, axis=1, keepdims=True) + epsilon)
    return (values * (scale * (1.0 / math.sqrt(cells.shape[1])))).astype(bf16)


def diagonal(size):
    return lax.broadcasted_iota(jnp.int32, (size, size), 0) == lax.broadcasted_iota(
        jnp.int32, (size, size), 1
    )


def upright(row, eye):
    return jnp.sum(jnp.where(eye, row, 0.0), axis=1, keepdims=True)


def affinity(col_unit, row_unit, col_mean, row_mean):
    scores = nt(col_unit, row_unit)
    return jnp.exp((2.0 * sharpness) * scores / (col_mean + row_mean))


def weighted(scores, col_mean, row_mean):
    return jnp.exp((2.0 * sharpness) * scores / (col_mean + row_mean)).astype(bf16)


def with_ones(narrow):
    return jnp.concatenate([narrow, jnp.ones((ONES, narrow.shape[1]), bf16)], axis=0)


def pieces(values):
    first = values.astype(bf16)
    rest = values - first.astype(f32)
    second = rest.astype(bf16)
    third = (rest - second.astype(f32)).astype(bf16)
    return jnp.concatenate([first, second, third], axis=0)


def joined(product, size):
    return product[:size] + (product[size : 2 * size] + product[2 * size :])


def inverse_factor(gram):
    size = gram.shape[0]
    tile, step = 8, 4
    count = size // tile
    eye = jnp.where(diagonal(size), 1.0, 0.0).astype(f32)
    table = jnp.concatenate([gram, eye], axis=1)
    parts = [table[g * tile : (g + 1) * tile] for g in range(count)]
    shape = (tile, 2 * size)
    place = lax.broadcasted_iota(jnp.int32, shape, 0)

    def wide(piece):
        return jnp.broadcast_to(piece, shape)

    def spread(first):
        return [
            {g: wide(parts[g][:, k : k + 1]) for g in range(k // tile, count)}
            for k in range(first, min(first + step, size))
        ]

    scales = [jnp.ones(shape, f32) for _ in range(count)]
    columns = spread(0) + spread(step)
    for first in range(0, size, step):
        for t in range(step):
            b, at = (first + t) // tile, (first + t) % tile
            scale = lax.rsqrt(wide(columns[t][b][at : at + 1]))
            scales[b] = jnp.where(place == at, scale, scales[b])
            factor = {g: column * scale for g, column in columns[t].items()}
            for u in range(t + 1, len(columns)):
                g, r = (first + u) // tile, (first + u) % tile
                ahead = wide(columns[t][g][r : r + 1]) * scale
                columns[u] = {g: c - factor[g] * ahead for g, c in columns[u].items()}
            factor[b] = jnp.where(place > at, factor[b], 0.0)
            row = wide(parts[b][at : at + 1]) * scale
            for g in range(b, count):
                parts[g] = parts[g] - factor[g] * row
        columns = columns[step:] + spread(first + 2 * step)
    return jnp.concatenate([(p * s)[:, size:] for p, s in zip(parts, scales)], axis=0)


def times(left, right):
    return jnp.dot(left, right, precision=HIGHEST, preferred_element_type=f32)


def gram_of(blocks, total):
    acc = None
    for block in blocks:
        term = lax.dot_general(
            block, block, (((1,), (1,)), ((), ())), precision=HIGHEST, preferred_element_type=f32
        )
        acc = term if acc is None else acc + term
    return acc * (1.0 / total)


def block_of(lane, d):
    return pl.ds(pl.multiple_of((lane ^ d) * BLOCK, BLOCK), BLOCK)


def vector_kernel(lanes, knn_ref, start_ref, mean_ref, left_ref):
    lane = lax.axis_index("cols")
    knn = knn_ref[...].astype(f32)
    mean_ref[...] = jnp.concatenate([knn[k : k + 1] for k in range(knn.shape[0])], axis=1)
    for d in range(lanes):
        left_ref[d] = with_ones(start_ref[:, block_of(lane, d)].astype(bf16))


def prep_kernel(lanes, mean_ref, left_ref, *refs):
    lists, (side_ref, mask_ref) = refs[:lanes], refs[lanes:]
    lane = lax.axis_index("cols")
    group = lax.axis_index("rows")
    blocks = lax.axis_size("rows") * lanes
    size = left_ref.shape[1] - ONES
    stride = 4 * blocks
    slot = lax.broadcasted_iota(jnp.int32, (1, lists[0].shape[1]), 1)
    codes = [
        jnp.where(slot < ref[2:3, 0:1], ref[0:1] * stride + ref[1:2], -stride) for ref in lists
    ]
    codes = jnp.concatenate(codes, axis=0)

    def live(row_block, col_block):
        hit = jnp.where(codes == row_block * stride + col_block, 1.0, 0.0)
        hit = jnp.max(jnp.max(hit, axis=1, keepdims=True), axis=0, keepdims=True)
        return jnp.broadcast_to(hit, (1, BLOCK))

    mine = group * lanes + lane
    rows = [group * lanes + (lane ^ d) for d in range(lanes)]
    masks = [live(row, mine) for row in rows] + [live(row, mine - lanes) for row in rows]
    mask_ref[...] = jnp.concatenate(masks, axis=0)
    back = [live(mine, row + lanes) for row in rows]
    means = mean_ref[:, block_of(lane, 0)]
    pad = jnp.zeros((ONES - lanes - 1, BLOCK), f32)
    after = jnp.concatenate([means, *back, pad], axis=0).astype(bf16)
    side_ref[...] = jnp.concatenate([left_ref[0, :size, :], after], axis=0)


def own_kernel(lanes, cells_ref, mean_ref, left_ref, unit_ref, weight_ref, product_ref):
    lane = lax.axis_index("cols")
    eye = diagonal(BLOCK)
    col_mean = upright(mean_ref[:, block_of(lane, 0)], eye)
    left = left_ref[0]
    rows = product_ref.shape[1]
    for d in range(lanes):
        unit = unit_rows(cells_ref[block_of(lane, d), :])
        unit_ref[d] = unit
        if d == 0:
            own = unit
        weights = affinity(own, unit, col_mean, mean_ref[:, block_of(lane, d)])
        if d == 0:
            weights = jnp.where(eye, 0.0, weights)
        weights = weights.astype(bf16)
        weight_ref[d] = weights
        product_ref[d] = jnp.dot(left, weights, preferred_element_type=f32)[:rows]


def scores_kernel(lanes, unit_ref, cells_ref, scores_ref):
    col_unit = unit_rows(cells_ref[...])
    for d in range(lanes):
        scores_ref[d] = nt(col_unit, unit_ref[d])


def next_kernel(lanes, *refs):
    scores_ref, side_ref, mean_ref, left_ref, own_ref, mask_ref, *outs = refs
    weight_ref, keep_ref, *core_refs, back_ref = outs
    lane = lax.axis_index("cols")
    size = left_ref.shape[1] - ONES
    after = side_ref[size:, :].astype(f32)
    col_mean = upright(after[0:1], diagonal(BLOCK))
    left = with_ones(side_ref[:size, :])
    rows = own_ref.shape[1]
    back = jnp.zeros((rows, BLOCK), f32)
    for d in range(lanes):
        weights = weighted(scores_ref[d], col_mean, mean_ref[:, block_of(lane, d)])
        weight_ref[d] = weights
        product = jnp.dot(left, weights, preferred_element_type=f32)[:rows]
        own = mask_ref[d : d + 1, :] * own_ref[d]
        halves(d, keep_ref, core_refs)[...] = own + mask_ref[lanes + d : lanes + d + 1, :] * product
        back = back + after[1 + d : 2 + d] * nt(left_ref[d], weights)[:rows]
    back_ref[...] = back


def halves(d, keep_ref, core_refs):
    return core_refs[d // 2] if d % 2 else keep_ref.at[d // 2]


def added(refs):
    total = refs[0][...]
    for ref in refs[1:]:
        total = total + ref[...]
    return total


def chip_kernel(keep_ref, back_ref, *refs):
    *came_refs, out_ref = refs
    rows = out_ref.shape[1]
    for m, came_ref in enumerate(came_refs):
        total = keep_ref[m] + came_ref[...]
        out_ref[m] = total + back_ref[:rows] if m == 0 else total


def pair_kernel(keep_ref, *refs):
    *came_refs, own_ref, away_ref = refs
    own_ref[...] = keep_ref[0] + came_refs[0][...]
    away_ref[...] = keep_ref[1] + came_refs[1][...]


def smooth_kernel(size, *refs):
    *parts, lead_ref, out_ref, wide_ref = refs
    total = added(parts)
    degree = total[size : size + 1]
    smooth = total[:size] / degree
    lead_ref[...] = smooth
    out_ref[:size] = smooth
    out_ref[size:] = jnp.broadcast_to(degree, (out_ref.shape[0] - size, BLOCK))
    wide_ref[:size] = smooth
    wide_ref[size:] = jnp.zeros((wide_ref.shape[0] - size, BLOCK), f32)


def back_kernel(lanes, total, weight_ref, side_ref, *refs):
    *block_refs, back_ref, gram_ref = refs
    size = gram_ref.shape[0]
    blocks = [ref[:size] for ref in block_refs]
    masks = side_ref[size:, :].astype(f32)
    back = jnp.zeros((size, BLOCK), f32)
    for d in range(lanes):
        left = pieces(blocks[d])
        back = back + masks[1 + d : 2 + d] * joined(nt(left, weight_ref[d]), size)
    back_ref[:size] = back
    back_ref[size:] = jnp.zeros((back_ref.shape[0] - size, BLOCK), f32)
    gram_ref[...] = gram_of(blocks, total)


def ordered(here_ref, there_ref):
    return [ref[m] for m in range(here_ref.shape[0]) for ref in (here_ref, there_ref)]


def forward_kernel(lanes, own_ref, weight_ref, mask_ref, lead_ref, next_ref, keep_ref, *core_refs):
    size = lead_ref.shape[0]
    own_left = pieces(lead_ref[...])
    next_left = pieces(next_ref[:size])
    for d in range(lanes):
        own = joined(jnp.dot(own_left, own_ref[d], preferred_element_type=f32), size)
        after = joined(jnp.dot(next_left, weight_ref[d], preferred_element_type=f32), size)
        own = mask_ref[d : d + 1, :] * own
        halves(d, keep_ref, core_refs)[...] = own + mask_ref[lanes + d : lanes + d + 1, :] * after


def resmooth_kernel(own_ref, came_ref, block_ref, across_ref, out_ref):
    size = out_ref.shape[1]
    for m, ref in enumerate((block_ref, across_ref)):
        out_ref[m] = (own_ref[m] + came_ref[1 - m]) / ref[size : size + 1]


def grams_kernel(total, first_ref, here_ref, there_ref, grams_ref):
    second = gram_of(ordered(here_ref, there_ref), total)
    grams_ref[...] = jnp.concatenate([first_ref[...], second], axis=1)


def solve_kernel(lanes, here_ref, there_ref, *refs):
    *grams, out_ref = refs
    lane = lax.axis_index("cols")
    size = out_ref.shape[0]
    both = added(grams)
    first = inverse_factor(both[:, :size])
    solved = [times(first, block) for block in ordered(here_ref, there_ref)]
    half = times(first, both[:, size:])
    gram = lax.dot_general(
        half, first, (((1,), (1,)), ((), ())), precision=HIGHEST, preferred_element_type=f32
    )
    second = inverse_factor(gram)
    for d in range(lanes):
        out_ref[:, block_of(lane, d)] = times(second, solved[d])


def call(body, outs, *args):
    vmem = pl.BlockSpec(memory_space=pltpu.VMEM)
    return pl.pallas_call(
        body,
        out_shape=[jax.ShapeDtypeStruct(shape, kind) for shape, kind in outs],
        in_specs=[vmem] * len(args),
        out_specs=[vmem] * len(outs),
        compiler_params=pltpu.CompilerParams(vmem_limit_bytes=40 * 1024 * 1024),
    )(*args)


def local(embeddings, knn_mean, pair_rows, pair_cols, pair_count, start_block):
    rows_here, width = embeddings.shape
    size = start_block.shape[0]
    slots = pair_rows.shape[2]
    lanes = lax.axis_size("cols")
    lane = lax.axis_index("cols")
    groups = lax.axis_size("rows")
    total = rows_here * groups
    assert rows_here == lanes * BLOCK and lanes == 4 and groups & (groups - 1) == 0
    wide = size + 8

    next_cells = shift(lax.dynamic_slice_in_dim(embeddings, lane * BLOCK, BLOCK, 0), 1)
    counts = jnp.pad(pair_count, ((0, 0), (0, slots - 1)))
    mine = jnp.concatenate([pair_rows[0], pair_cols[0], counts], axis=0)
    mean, left = call(
        functools.partial(vector_kernel, lanes),
        [((1, rows_here), f32), ((lanes, size + ONES, BLOCK), bf16)],
        knn_mean.reshape(rows_here // 128, 128),
        start_block,
    )
    side, masks = call(
        functools.partial(prep_kernel, lanes),
        [((size + ONES, BLOCK), bf16), ((2 * lanes, BLOCK), f32)],
        mean,
        left,
        *lane_swaps(mine),
    )
    next_side = shift(side, 1)

    unit, own_weights, own_product = call(
        functools.partial(own_kernel, lanes),
        [
            ((lanes, BLOCK, width), bf16),
            ((lanes, BLOCK, BLOCK), bf16),
            ((lanes, wide, BLOCK), f32),
        ],
        embeddings,
        mean,
        left,
    )
    (scores,) = call(
        functools.partial(scores_kernel, lanes), [((lanes, BLOCK, BLOCK), f32)], unit, next_cells
    )
    next_weights, keep, *core, back = call(
        functools.partial(next_kernel, lanes),
        [((lanes, BLOCK, BLOCK), bf16), ((lanes // 2, wide, BLOCK), f32)]
        + [((wide, BLOCK), f32)] * (lanes // 2 + 1),
        scores,
        next_side,
        mean,
        left,
        own_product,
        masks,
    )

    came = [swap(part, "cols", 1) for part in core]
    own, away = call(pair_kernel, [((wide, BLOCK), f32)] * 2, keep, *came)
    lead, smooth, wider = call(
        functools.partial(smooth_kernel, size),
        [((size, BLOCK), f32), ((wide, BLOCK), f32), ((wide + 8, BLOCK), f32)],
        own,
        swap(away, "cols", 2),
        shift(back, -1),
    )

    after = shift(wider, 1)
    across = swap(smooth, "cols", 2)
    back, gram = call(
        functools.partial(back_kernel, lanes, total),
        [((wide, BLOCK), f32), ((size, size), f32)],
        next_weights,
        next_side,
        lead,
        swap(lead, "cols", 1),
        across,
        swap(across, "cols", 1),
    )
    masks, gram = lax.optimization_barrier((masks, gram))
    keep, *core = call(
        functools.partial(forward_kernel, lanes),
        [((lanes // 2, size, BLOCK), f32)] + [((size, BLOCK), f32)] * (lanes // 2),
        own_weights,
        next_weights,
        masks,
        lead,
        after,
    )
    came = [swap(part, "cols", 1) for part in core]
    (both,) = call(chip_kernel, [(keep.shape, f32)], keep, shift(back, -1, around=False), *came)
    (here,) = call(
        resmooth_kernel,
        [((lanes // 2, size, BLOCK), f32)],
        both,
        swap(both, "cols", 2),
        smooth,
        across,
    )
    there = swap(here, "cols", 1)
    (grams,) = call(
        functools.partial(grams_kernel, total), [((size, 2 * size), f32)], gram, here, there
    )
    (vector,) = call(
        functools.partial(solve_kernel, lanes),
        [((size, rows_here), f32)],
        here,
        there,
        *all_rows(grams),
    )
    return vector


def solution(mesh):
    in_specs = (
        P("rows", None),
        P("rows"),
        P("rows", "cols", None),
        P("rows", "cols", None),
        P("rows", "cols"),
        P(None, "rows"),
    )
    out_specs = P(None, "rows")
    return jax.shard_map(local, mesh=mesh, in_specs=in_specs, out_specs=out_specs, check_vma=False)
```

```python
import functools
import math

import jax
import jax.numpy as jnp
from jax import lax
from jax.experimental import pallas as pl
from jax.experimental.pallas import tpu as pltpu
from jax.sharding import PartitionSpec as P

BLOCK = 256
ONES = 16

sharpness = 10.0
epsilon = 1e-06

HIGHEST = lax.Precision.HIGHEST
f32 = jnp.float32
bf16 = jnp.bfloat16


def shift(cells, step, around=True):
    count = lax.axis_size("rows")
    pairs = [(i, (i + step) % count) for i in range(count) if around or 0 <= i + step < count]
    return lax.ppermute(cells, "rows", pairs)


def swap(cells, axis, offset):
    count = lax.axis_size(axis)
    return lax.ppermute(cells, axis, [(i, i ^ offset) for i in range(count)])


def lane_swaps(cells):
    return [cells] + [swap(cells, "cols", d) for d in range(1, lax.axis_size("cols"))]


def both_swap(cells, row_offset, lane_offset):
    groups, lanes = lax.axis_size("rows"), lax.axis_size("cols")
    pairs = [
        (r * lanes + lane, (r ^ row_offset) * lanes + (lane ^ lane_offset))
        for r in range(groups)
        for lane in range(lanes)
    ]
    return lax.ppermute(cells, ("rows", "cols"), pairs)


def nt(left, right):
    return lax.dot_general(left, right, (((1,), (1,)), ((), ())), preferred_element_type=f32)


def unit_rows(cells):
    values = cells.astype(f32)
    scale = lax.rsqrt(jnp.mean(values * values, axis=1, keepdims=True) + epsilon)
    return (values * (scale * (1.0 / math.sqrt(cells.shape[1])))).astype(bf16)


def diagonal(size):
    return lax.broadcasted_iota(jnp.int32, (size, size), 0) == lax.broadcasted_iota(
        jnp.int32, (size, size), 1
    )


def upright(row, eye):
    return jnp.sum(jnp.where(eye, row, 0.0), axis=1, keepdims=True)


def affinity(col_unit, row_unit, col_mean, row_mean):
    scores = nt(col_unit, row_unit)
    return jnp.exp((2.0 * sharpness) * scores / (col_mean + row_mean))


def weighted(scores, col_mean, row_mean):
    return jnp.exp((2.0 * sharpness) * scores / (col_mean + row_mean)).astype(bf16)


def with_ones(narrow):
    return jnp.concatenate([narrow, jnp.ones((ONES, narrow.shape[1]), bf16)], axis=0)


def pieces(values):
    first = values.astype(bf16)
    rest = values - first.astype(f32)
    second = rest.astype(bf16)
    third = (rest - second.astype(f32)).astype(bf16)
    return jnp.concatenate([first, second, third], axis=0)


def joined(product, size):
    return product[:size] + (product[size : 2 * size] + product[2 * size :])


def inverse_factor(gram):
    size = gram.shape[0]
    tile, step = 8, 4
    count = size // tile
    eye = jnp.where(diagonal(size), 1.0, 0.0).astype(f32)
    table = jnp.concatenate([gram, eye], axis=1)
    parts = [table[g * tile : (g + 1) * tile] for g in range(count)]
    shape = (tile, 2 * size)
    place = lax.broadcasted_iota(jnp.int32, shape, 0)

    def wide(piece):
        return jnp.broadcast_to(piece, shape)

    def spread(first):
        return [
            {g: wide(parts[g][:, k : k + 1]) for g in range(k // tile, count)}
            for k in range(first, min(first + step, size))
        ]

    scales = [jnp.ones(shape, f32) for _ in range(count)]
    columns = spread(0) + spread(step)
    for first in range(0, size, step):
        for t in range(step):
            b, at = (first + t) // tile, (first + t) % tile
            scale = lax.rsqrt(wide(columns[t][b][at : at + 1]))
            scales[b] = jnp.where(place == at, scale, scales[b])
            factor = {g: column * scale for g, column in columns[t].items()}
            for u in range(t + 1, len(columns)):
                g, r = (first + u) // tile, (first + u) % tile
                ahead = wide(columns[t][g][r : r + 1]) * scale
                columns[u] = {g: c - factor[g] * ahead for g, c in columns[u].items()}
            factor[b] = jnp.where(place > at, factor[b], 0.0)
            row = wide(parts[b][at : at + 1]) * scale
            for g in range(b, count):
                parts[g] = parts[g] - factor[g] * row
        columns = columns[step:] + spread(first + 2 * step)
    return jnp.concatenate([(p * s)[:, size:] for p, s in zip(parts, scales)], axis=0)


def times(left, right):
    return jnp.dot(left, right, precision=HIGHEST, preferred_element_type=f32)


def gram_of(blocks, total):
    acc = None
    for block in blocks:
        term = lax.dot_general(
            block, block, (((1,), (1,)), ((), ())), precision=HIGHEST, preferred_element_type=f32
        )
        acc = term if acc is None else acc + term
    return acc * (1.0 / total)


def block_of(lane, d):
    return pl.ds(pl.multiple_of((lane ^ d) * BLOCK, BLOCK), BLOCK)


def vector_kernel(lanes, knn_ref, start_ref, mean_ref, left_ref):
    lane = lax.axis_index("cols")
    knn = knn_ref[...].astype(f32)
    mean_ref[...] = jnp.concatenate([knn[k : k + 1] for k in range(knn.shape[0])], axis=1)
    for d in range(lanes):
        left_ref[d] = with_ones(start_ref[:, block_of(lane, d)].astype(bf16))


def prep_kernel(lanes, mean_ref, left_ref, *refs):
    lists, (side_ref, mask_ref) = refs[:lanes], refs[lanes:]
    lane = lax.axis_index("cols")
    group = lax.axis_index("rows")
    blocks = lax.axis_size("rows") * lanes
    size = left_ref.shape[1] - ONES
    stride = 4 * blocks
    slot = lax.broadcasted_iota(jnp.int32, (1, lists[0].shape[1]), 1)
    codes = [
        jnp.where(slot < ref[2:3, 0:1], ref[0:1] * stride + ref[1:2], -stride) for ref in lists
    ]
    codes = jnp.concatenate(codes, axis=0)

    def live(row_block, col_block):
        hit = jnp.where(codes == row_block * stride + col_block, 1.0, 0.0)
        hit = jnp.max(jnp.max(hit, axis=1, keepdims=True), axis=0, keepdims=True)
        return jnp.broadcast_to(hit, (1, BLOCK))

    mine = group * lanes + lane
    rows = [group * lanes + (lane ^ d) for d in range(lanes)]
    masks = [live(row, mine) for row in rows] + [live(row, mine - lanes) for row in rows]
    mask_ref[...] = jnp.concatenate(masks, axis=0)
    back = [live(mine, row + lanes) for row in rows]
    means = mean_ref[:, block_of(lane, 0)]
    pad = jnp.zeros((ONES - lanes - 1, BLOCK), f32)
    after = jnp.concatenate([means, *back, pad], axis=0).astype(bf16)
    side_ref[...] = jnp.concatenate([left_ref[0, :size, :], after], axis=0)


def own_kernel(lanes, cells_ref, mean_ref, left_ref, unit_ref, weight_ref, product_ref):
    lane = lax.axis_index("cols")
    eye = diagonal(BLOCK)
    col_mean = upright(mean_ref[:, block_of(lane, 0)], eye)
    left = left_ref[0]
    rows = product_ref.shape[1]
    for d in range(lanes):
        unit = unit_rows(cells_ref[block_of(lane, d), :])
        unit_ref[d] = unit
        if d == 0:
            own = unit
        weights = affinity(own, unit, col_mean, mean_ref[:, block_of(lane, d)])
        if d == 0:
            weights = jnp.where(eye, 0.0, weights)
        weights = weights.astype(bf16)
        weight_ref[d] = weights
        product_ref[d] = jnp.dot(left, weights, preferred_element_type=f32)[:rows]


def scores_kernel(lanes, unit_ref, cells_ref, scores_ref):
    col_unit = unit_rows(cells_ref[...])
    for d in range(lanes):
        scores_ref[d] = nt(col_unit, unit_ref[d])


def next_kernel(lanes, *refs):
    scores_ref, side_ref, mean_ref, left_ref, own_ref, mask_ref, *outs = refs
    weight_ref, keep_ref, *core_refs, back_ref = outs
    lane = lax.axis_index("cols")
    size = left_ref.shape[1] - ONES
    after = side_ref[size:, :].astype(f32)
    col_mean = upright(after[0:1], diagonal(BLOCK))
    left = with_ones(side_ref[:size, :])
    rows = own_ref.shape[1]
    back = jnp.zeros((rows, BLOCK), f32)
    for d in range(lanes):
        weights = weighted(scores_ref[d], col_mean, mean_ref[:, block_of(lane, d)])
        weight_ref[d] = weights
        product = jnp.dot(left, weights, preferred_element_type=f32)[:rows]
        own = mask_ref[d : d + 1, :] * own_ref[d]
        halves(d, keep_ref, core_refs)[...] = own + mask_ref[lanes + d : lanes + d + 1, :] * product
        back = back + after[1 + d : 2 + d] * nt(left_ref[d], weights)[:rows]
    back_ref[...] = back


def halves(d, keep_ref, core_refs):
    return core_refs[d // 2] if d % 2 else keep_ref.at[d // 2]


def added(refs):
    total = refs[0][...]
    for ref in refs[1:]:
        total = total + ref[...]
    return total


def chip_kernel(keep_ref, back_ref, *refs):
    *came_refs, out_ref = refs
    rows = out_ref.shape[1]
    for m, came_ref in enumerate(came_refs):
        total = keep_ref[m] + came_ref[...]
        out_ref[m] = total + back_ref[:rows] if m == 0 else total


def pair_kernel(keep_ref, *refs):
    *came_refs, own_ref, away_ref = refs
    own_ref[...] = keep_ref[0] + came_refs[0][...]
    away_ref[...] = keep_ref[1] + came_refs[1][...]


def smooth_kernel(size, *refs):
    *parts, lead_ref, out_ref, wide_ref = refs
    total = added(parts)
    degree = total[size : size + 1]
    smooth = total[:size] / degree
    lead_ref[...] = smooth
    out_ref[:size] = smooth
    out_ref[size:] = jnp.broadcast_to(degree, (out_ref.shape[0] - size, BLOCK))
    wide_ref[:size] = smooth
    wide_ref[size:] = jnp.zeros((wide_ref.shape[0] - size, BLOCK), f32)


def back_kernel(lanes, total, weight_ref, side_ref, *refs):
    *block_refs, back_ref, gram_ref = refs
    size = gram_ref.shape[0]
    blocks = [ref[:size] for ref in block_refs]
    masks = side_ref[size:, :].astype(f32)
    back = jnp.zeros((size, BLOCK), f32)
    for d in range(lanes):
        left = pieces(blocks[d])
        back = back + masks[1 + d : 2 + d] * joined(nt(left, weight_ref[d]), size)
    back_ref[:size] = back
    back_ref[size:] = jnp.zeros((back_ref.shape[0] - size, BLOCK), f32)
    gram_ref[...] = gram_of(blocks[::2], total)


def ordered(here_ref, there_ref):
    return [ref[m] for m in range(here_ref.shape[0]) for ref in (here_ref, there_ref)]


def forward_kernel(lanes, own_ref, weight_ref, mask_ref, lead_ref, next_ref, keep_ref, *core_refs):
    size = lead_ref.shape[0]
    own_left = pieces(lead_ref[...])
    next_left = pieces(next_ref[:size])
    for d in range(lanes):
        own = joined(jnp.dot(own_left, own_ref[d], preferred_element_type=f32), size)
        after = joined(jnp.dot(next_left, weight_ref[d], preferred_element_type=f32), size)
        own = mask_ref[d : d + 1, :] * own
        halves(d, keep_ref, core_refs)[...] = own + mask_ref[lanes + d : lanes + d + 1, :] * after


def resmooth_kernel(total, first_ref, own_ref, came_ref, block_ref, across_ref, out_ref, *grams_refs):
    size = out_ref.shape[1]
    blocks = []
    for m, ref in enumerate((block_ref, across_ref)):
        blocks.append((own_ref[m] + came_ref[1 - m]) / ref[size : size + 1])
        out_ref[m] = blocks[m]
    spread_out(jnp.concatenate([first_ref[...], gram_of(blocks, total)], axis=1), grams_refs)


def spread_out(value, refs):
    rows = value.shape[0]
    for ref in refs:
        ref[:rows] = value
        if ref.shape[0] > rows:
            ref[rows:] = jnp.zeros((ref.shape[0] - rows, ref.shape[1]), f32)


def sum_kernel(count, *refs):
    parts, outs = refs[:count], refs[count:]
    rows = outs[0].shape[0]
    total = parts[0][:rows]
    for part in parts[1:]:
        total = total + part[:rows]
    spread_out(total, outs)


def solve_kernel(lanes, here_ref, there_ref, *refs):
    *grams, out_ref = refs
    lane = lax.axis_index("cols")
    size = out_ref.shape[0]
    both = grams[0][:size]
    for part in grams[1:]:
        both = both + part[:size]
    first = inverse_factor(both[:, :size])
    solved = [times(first, block) for block in ordered(here_ref, there_ref)]
    half = times(first, both[:, size:])
    gram = lax.dot_general(
        half, first, (((1,), (1,)), ((), ())), precision=HIGHEST, preferred_element_type=f32
    )
    second = inverse_factor(gram)
    for d in range(lanes):
        out_ref[:, block_of(lane, d)] = times(second, solved[d])


def call(body, outs, *args):
    vmem = pl.BlockSpec(memory_space=pltpu.VMEM)
    return pl.pallas_call(
        body,
        out_shape=[jax.ShapeDtypeStruct(shape, kind) for shape, kind in outs],
        in_specs=[vmem] * len(args),
        out_specs=[vmem] * len(outs),
        compiler_params=pltpu.CompilerParams(vmem_limit_bytes=40 * 1024 * 1024),
    )(*args)


def local(embeddings, knn_mean, pair_rows, pair_cols, pair_count, start_block):
    rows_here, width = embeddings.shape
    size = start_block.shape[0]
    slots = pair_rows.shape[2]
    lanes = lax.axis_size("cols")
    lane = lax.axis_index("cols")
    groups = lax.axis_size("rows")
    total = rows_here * groups
    assert rows_here == lanes * BLOCK and lanes == 4 and groups & (groups - 1) == 0
    wide = size + 8

    next_cells = shift(lax.dynamic_slice_in_dim(embeddings, lane * BLOCK, BLOCK, 0), 1)
    counts = jnp.pad(pair_count, ((0, 0), (0, slots - 1)))
    mine = jnp.concatenate([pair_rows[0], pair_cols[0], counts], axis=0)
    mean, left = call(
        functools.partial(vector_kernel, lanes),
        [((1, rows_here), f32), ((lanes, size + ONES, BLOCK), bf16)],
        knn_mean.reshape(rows_here // 128, 128),
        start_block,
    )
    side, masks = call(
        functools.partial(prep_kernel, lanes),
        [((size + ONES, BLOCK), bf16), ((2 * lanes, BLOCK), f32)],
        mean,
        left,
        *lane_swaps(mine),
    )
    next_side = shift(side, 1)

    unit, own_weights, own_product = call(
        functools.partial(own_kernel, lanes),
        [
            ((lanes, BLOCK, width), bf16),
            ((lanes, BLOCK, BLOCK), bf16),
            ((lanes, wide, BLOCK), f32),
        ],
        embeddings,
        mean,
        left,
    )
    (scores,) = call(
        functools.partial(scores_kernel, lanes), [((lanes, BLOCK, BLOCK), f32)], unit, next_cells
    )
    next_weights, keep, *core, back = call(
        functools.partial(next_kernel, lanes),
        [((lanes, BLOCK, BLOCK), bf16), ((lanes // 2, wide, BLOCK), f32)]
        + [((wide, BLOCK), f32)] * (lanes // 2 + 1),
        scores,
        next_side,
        mean,
        left,
        own_product,
        masks,
    )

    came = [swap(part, "cols", 1) for part in core]
    own, away = call(pair_kernel, [((wide, BLOCK), f32)] * 2, keep, *came)
    lead, smooth, wider = call(
        functools.partial(smooth_kernel, size),
        [((size, BLOCK), f32), ((wide, BLOCK), f32), ((wide + 8, BLOCK), f32)],
        own,
        swap(away, "cols", 2),
        shift(back, -1),
    )

    after = shift(wider, 1)
    across = swap(smooth, "cols", 2)
    back, gram = call(
        functools.partial(back_kernel, lanes, total),
        [((wide, BLOCK), f32), ((size, size), f32)],
        next_weights,
        next_side,
        lead,
        swap(lead, "cols", 1),
        across,
        swap(across, "cols", 1),
    )
    masks, gram = lax.optimization_barrier((masks, gram))
    keep, *core = call(
        functools.partial(forward_kernel, lanes),
        [((lanes // 2, size, BLOCK), f32)] + [((size, BLOCK), f32)] * (lanes // 2),
        own_weights,
        next_weights,
        masks,
        lead,
        after,
    )
    came = [swap(part, "cols", 1) for part in core]
    (both,) = call(chip_kernel, [(keep.shape, f32)], keep, shift(back, -1, around=False), *came)
    tall = [((size + 8 * k, 2 * size), f32) for k in range(3)]
    here, *grams = call(
        functools.partial(resmooth_kernel, total),
        [((lanes // 2, size, BLOCK), f32), *tall],
        gram,
        both,
        swap(both, "cols", 2),
        smooth,
        across,
    )

    bits = groups.bit_length() - 1
    low = bits % 2
    parts = [grams[0], swap(grams[0], "cols", 1)]
    if low:
        parts += [swap(grams[1], "rows", 1), both_swap(grams[2], 1, 1)]
    while low < bits:
        grams = call(functools.partial(sum_kernel, len(parts)), tall, *parts)
        if low < 2:
            here, grams = lax.optimization_barrier((here, grams))
        parts = [grams[0]] + [swap(grams[m - 1], "rows", m << low) for m in (1, 2, 3)]
        low += 2
    (vector,) = call(
        functools.partial(solve_kernel, lanes),
        [((size, rows_here), f32)],
        here,
        swap(here, "cols", 1),
        *parts,
    )
    return vector


def solution(mesh):
    in_specs = (
        P("rows", None),
        P("rows"),
        P("rows", "cols", None),
        P("rows", "cols", None),
        P("rows", "cols"),
        P(None, "rows"),
    )
    out_specs = P(None, "rows")
    return jax.shard_map(local, mesh=mesh, in_specs=in_specs, out_specs=out_specs, check_vma=False)
```

```python
import functools
import math

import jax
import jax.numpy as jnp
from jax import lax
from jax.experimental import pallas as pl
from jax.experimental.pallas import tpu as pltpu
from jax.sharding import PartitionSpec as P

BLOCK = 256
ONES = 16

sharpness = 10.0
epsilon = 1e-06

HIGHEST = lax.Precision.HIGHEST
f32 = jnp.float32
bf16 = jnp.bfloat16


def shift(cells, step, around=True):
    count = lax.axis_size("rows")
    pairs = [(i, (i + step) % count) for i in range(count) if around or 0 <= i + step < count]
    return lax.ppermute(cells, "rows", pairs)


def swap(cells, axis, offset):
    count = lax.axis_size(axis)
    return lax.ppermute(cells, axis, [(i, i ^ offset) for i in range(count)])


def lane_swaps(cells):
    return [cells] + [swap(cells, "cols", d) for d in range(1, lax.axis_size("cols"))]


def both_swap(cells, row_offset, lane_offset):
    groups, lanes = lax.axis_size("rows"), lax.axis_size("cols")
    pairs = [
        (r * lanes + lane, (r ^ row_offset) * lanes + (lane ^ lane_offset))
        for r in range(groups)
        for lane in range(lanes)
    ]
    return lax.ppermute(cells, ("rows", "cols"), pairs)


def nt(left, right):
    return lax.dot_general(left, right, (((1,), (1,)), ((), ())), preferred_element_type=f32)


def unit_rows(cells):
    values = cells.astype(f32)
    scale = lax.rsqrt(jnp.mean(values * values, axis=1, keepdims=True) + epsilon)
    return (values * (scale * (1.0 / math.sqrt(cells.shape[1])))).astype(bf16)


def diagonal(size):
    return lax.broadcasted_iota(jnp.int32, (size, size), 0) == lax.broadcasted_iota(
        jnp.int32, (size, size), 1
    )


def upright(row, eye):
    return jnp.sum(jnp.where(eye, row, 0.0), axis=1, keepdims=True)


def affinity(col_unit, row_unit, col_mean, row_mean):
    scores = nt(col_unit, row_unit)
    return jnp.exp((2.0 * sharpness) * scores / (col_mean + row_mean))


def weighted(scores, col_mean, row_mean):
    return jnp.exp((2.0 * sharpness) * scores / (col_mean + row_mean)).astype(bf16)


def with_ones(narrow):
    return jnp.concatenate([narrow, jnp.ones((ONES, narrow.shape[1]), bf16)], axis=0)


def pieces(values):
    first = values.astype(bf16)
    rest = values - first.astype(f32)
    second = rest.astype(bf16)
    third = (rest - second.astype(f32)).astype(bf16)
    return jnp.concatenate([first, second, third], axis=0)


def joined(product, size):
    return product[:size] + (product[size : 2 * size] + product[2 * size :])


def inverse_factor(gram):
    size = gram.shape[0]
    tile, step = 8, 4
    count = size // tile
    eye = jnp.where(diagonal(size), 1.0, 0.0).astype(f32)
    table = jnp.concatenate([gram, eye], axis=1)
    parts = [table[g * tile : (g + 1) * tile] for g in range(count)]
    shape = (tile, 2 * size)
    place = lax.broadcasted_iota(jnp.int32, shape, 0)

    def wide(piece):
        return jnp.broadcast_to(piece, shape)

    def spread(first):
        return [
            {g: wide(parts[g][:, k : k + 1]) for g in range(k // tile, count)}
            for k in range(first, min(first + step, size))
        ]

    scales = [jnp.ones(shape, f32) for _ in range(count)]
    columns = spread(0) + spread(step)
    for first in range(0, size, step):
        for t in range(step):
            b, at = (first + t) // tile, (first + t) % tile
            scale = lax.rsqrt(wide(columns[t][b][at : at + 1]))
            scales[b] = jnp.where(place == at, scale, scales[b])
            factor = {g: column * scale for g, column in columns[t].items()}
            for u in range(t + 1, len(columns)):
                g, r = (first + u) // tile, (first + u) % tile
                ahead = wide(columns[t][g][r : r + 1]) * scale
                columns[u] = {g: c - factor[g] * ahead for g, c in columns[u].items()}
            factor[b] = jnp.where(place > at, factor[b], 0.0)
            row = wide(parts[b][at : at + 1]) * scale
            for g in range(b, count):
                parts[g] = parts[g] - factor[g] * row
        columns = columns[step:] + spread(first + 2 * step)
    return jnp.concatenate([(p * s)[:, size:] for p, s in zip(parts, scales)], axis=0)


def times(left, right):
    return jnp.dot(left, right, precision=HIGHEST, preferred_element_type=f32)


def gram_of(blocks, total):
    acc = None
    for block in blocks:
        term = lax.dot_general(
            block, block, (((1,), (1,)), ((), ())), precision=HIGHEST, preferred_element_type=f32
        )
        acc = term if acc is None else acc + term
    return acc * (1.0 / total)


def block_of(lane, d):
    return pl.ds(pl.multiple_of((lane ^ d) * BLOCK, BLOCK), BLOCK)


def vector_kernel(lanes, knn_ref, start_ref, mean_ref, left_ref):
    lane = lax.axis_index("cols")
    knn = knn_ref[...].astype(f32)
    mean_ref[...] = jnp.concatenate([knn[k : k + 1] for k in range(knn.shape[0])], axis=1)
    for d in range(lanes):
        left_ref[d] = with_ones(start_ref[:, block_of(lane, d)].astype(bf16))


def prep_kernel(lanes, mean_ref, left_ref, *refs):
    lists, (side_ref, mask_ref) = refs[:lanes], refs[lanes:]
    lane = lax.axis_index("cols")
    group = lax.axis_index("rows")
    blocks = lax.axis_size("rows") * lanes
    size = left_ref.shape[1] - ONES
    stride = 4 * blocks
    slot = lax.broadcasted_iota(jnp.int32, (1, lists[0].shape[1]), 1)
    codes = [
        jnp.where(slot < ref[2:3, 0:1], ref[0:1] * stride + ref[1:2], -stride) for ref in lists
    ]
    codes = jnp.concatenate(codes, axis=0)

    def live(row_block, col_block):
        hit = jnp.where(codes == row_block * stride + col_block, 1.0, 0.0)
        hit = jnp.max(jnp.max(hit, axis=1, keepdims=True), axis=0, keepdims=True)
        return jnp.broadcast_to(hit, (1, BLOCK))

    mine = group * lanes + lane
    rows = [group * lanes + (lane ^ d) for d in range(lanes)]
    masks = [live(row, mine) for row in rows] + [live(row, mine - lanes) for row in rows]
    mask_ref[...] = jnp.concatenate(masks, axis=0)
    back = [live(mine, row + lanes) for row in rows]
    means = mean_ref[:, block_of(lane, 0)]
    pad = jnp.zeros((ONES - lanes - 1, BLOCK), f32)
    after = jnp.concatenate([means, *back, pad], axis=0).astype(bf16)
    side_ref[...] = jnp.concatenate([left_ref[0, :size, :], after], axis=0)


def own_kernel(lanes, cells_ref, mean_ref, left_ref, unit_ref, weight_ref, product_ref):
    lane = lax.axis_index("cols")
    eye = diagonal(BLOCK)
    col_mean = upright(mean_ref[:, block_of(lane, 0)], eye)
    left = left_ref[0]
    rows = product_ref.shape[1]
    for d in range(lanes):
        unit = unit_rows(cells_ref[block_of(lane, d), :])
        unit_ref[d] = unit
        if d == 0:
            own = unit
        weights = affinity(own, unit, col_mean, mean_ref[:, block_of(lane, d)])
        if d == 0:
            weights = jnp.where(eye, 0.0, weights)
        weights = weights.astype(bf16)
        weight_ref[d] = weights
        product_ref[d] = jnp.dot(left, weights, preferred_element_type=f32)[:rows]


def scores_kernel(lanes, unit_ref, cells_ref, scores_ref):
    col_unit = unit_rows(cells_ref[...])
    for d in range(lanes):
        scores_ref[d] = nt(col_unit, unit_ref[d])


def next_kernel(lanes, *refs):
    scores_ref, side_ref, mean_ref, left_ref, own_ref, mask_ref, *outs = refs
    weight_ref, keep_ref, *core_refs, back_ref = outs
    lane = lax.axis_index("cols")
    size = left_ref.shape[1] - ONES
    after = side_ref[size:, :].astype(f32)
    col_mean = upright(after[0:1], diagonal(BLOCK))
    left = with_ones(side_ref[:size, :])
    rows = own_ref.shape[1]
    back = jnp.zeros((rows, BLOCK), f32)
    for d in range(lanes):
        weights = weighted(scores_ref[d], col_mean, mean_ref[:, block_of(lane, d)])
        weight_ref[d] = weights
        product = jnp.dot(left, weights, preferred_element_type=f32)[:rows]
        own = mask_ref[d : d + 1, :] * own_ref[d]
        halves(d, keep_ref, core_refs)[...] = own + mask_ref[lanes + d : lanes + d + 1, :] * product
        back = back + after[1 + d : 2 + d] * nt(left_ref[d], weights)[:rows]
    back_ref[...] = back


def halves(d, keep_ref, core_refs):
    return core_refs[d // 2] if d % 2 else keep_ref.at[d // 2]


def added(refs):
    total = refs[0][...]
    for ref in refs[1:]:
        total = total + ref[...]
    return total


def chip_kernel(keep_ref, back_ref, *refs):
    *came_refs, out_ref = refs
    rows = out_ref.shape[1]
    for m, came_ref in enumerate(came_refs):
        total = keep_ref[m] + came_ref[...]
        out_ref[m] = total + back_ref[:rows] if m == 0 else total


def pair_kernel(keep_ref, *refs):
    *came_refs, own_ref, away_ref = refs
    own_ref[...] = keep_ref[0] + came_refs[0][...]
    away_ref[...] = keep_ref[1] + came_refs[1][...]


def smooth_kernel(size, *refs):
    *parts, lead_ref, out_ref, wide_ref = refs
    total = added(parts)
    degree = total[size : size + 1]
    smooth = total[:size] / degree
    lead_ref[...] = smooth
    out_ref[:size] = smooth
    out_ref[size:] = jnp.broadcast_to(degree, (out_ref.shape[0] - size, BLOCK))
    wide_ref[:size] = smooth
    wide_ref[size:] = jnp.zeros((wide_ref.shape[0] - size, BLOCK), f32)


def back_kernel(lanes, total, weight_ref, side_ref, *refs):
    *block_refs, back_ref, gram_ref = refs
    size = gram_ref.shape[0]
    blocks = [ref[:size] for ref in block_refs]
    masks = side_ref[size:, :].astype(f32)
    back = jnp.zeros((size, BLOCK), f32)
    for d in range(lanes):
        left = pieces(blocks[d])
        back = back + masks[1 + d : 2 + d] * joined(nt(left, weight_ref[d]), size)
    back_ref[:size] = back
    back_ref[size:] = jnp.zeros((back_ref.shape[0] - size, BLOCK), f32)
    gram_ref[...] = gram_of(blocks[::2], total)


def ordered(here_ref, there_ref):
    return [ref[m] for m in range(here_ref.shape[0]) for ref in (here_ref, there_ref)]


def forward_kernel(lanes, own_ref, weight_ref, mask_ref, lead_ref, next_ref, keep_ref, *core_refs):
    size = lead_ref.shape[0]
    own_left = pieces(lead_ref[...])
    next_left = pieces(next_ref[:size])
    for d in range(lanes):
        own = joined(jnp.dot(own_left, own_ref[d], preferred_element_type=f32), size)
        after = joined(jnp.dot(next_left, weight_ref[d], preferred_element_type=f32), size)
        own = mask_ref[d : d + 1, :] * own
        halves(d, keep_ref, core_refs)[...] = own + mask_ref[lanes + d : lanes + d + 1, :] * after


def resmooth_kernel(total, first_ref, own_ref, came_ref, block_ref, across_ref, out_ref, *grams_refs):
    size = out_ref.shape[1]
    blocks = []
    for m, ref in enumerate((block_ref, across_ref)):
        blocks.append((own_ref[m] + came_ref[1 - m]) / ref[size : size + 1])
        out_ref[m] = blocks[m]
    spread_out(packed(first_ref[...], gram_of(blocks, total)), grams_refs)


def places(size):
    shape = (size, size)
    return lax.broadcasted_iota(jnp.int32, shape, 0), lax.broadcasted_iota(jnp.int32, shape, 1)


def packed(first, second):
    size = first.shape[0]
    row, column = places(size)
    mixed = jnp.where(row >= column, first, second)
    middle = size // 2
    edge = jnp.sum(jnp.where(row == column, second, 0.0), axis=0, keepdims=True)
    edge = jnp.broadcast_to(jnp.concatenate([edge, edge], axis=1), (8, 2 * size))
    return jnp.concatenate(
        [jnp.concatenate([mixed[:middle], mixed[middle:]], axis=1), edge], axis=0
    )


def unpacked(rows, size):
    row, column = places(size)
    middle = size // 2
    mixed = jnp.concatenate([rows[:middle, :size], rows[:middle, size:]], axis=0)
    flipped = mixed.T
    first = jnp.where(row >= column, mixed, flipped)
    second = jnp.where(row < column, mixed, flipped)
    return first, jnp.where(row == column, rows[middle : middle + 1, :size], second)


def spread_out(value, refs):
    rows = value.shape[0]
    for ref in refs:
        ref[:rows] = value
        if ref.shape[0] > rows:
            ref[rows:] = jnp.zeros((ref.shape[0] - rows, ref.shape[1]), f32)


def sum_kernel(count, *refs):
    parts, outs = refs[:count], refs[count:]
    rows = outs[0].shape[0]
    total = parts[0][:rows]
    for part in parts[1:]:
        total = total + part[:rows]
    spread_out(total, outs)


def solve_kernel(lanes, here_ref, there_ref, *refs):
    *grams, out_ref = refs
    lane = lax.axis_index("cols")
    size = out_ref.shape[0]
    rows = grams[0].shape[0]
    both = grams[0][...]
    for part in grams[1:]:
        both = both + part[:rows]
    one, two = unpacked(both, size)
    first = inverse_factor(one)
    solved = [times(first, block) for block in ordered(here_ref, there_ref)]
    half = times(first, two)
    gram = lax.dot_general(
        half, first, (((1,), (1,)), ((), ())), precision=HIGHEST, preferred_element_type=f32
    )
    second = inverse_factor(gram)
    for d in range(lanes):
        out_ref[:, block_of(lane, d)] = times(second, solved[d])


def call(body, outs, *args):
    vmem = pl.BlockSpec(memory_space=pltpu.VMEM)
    return pl.pallas_call(
        body,
        out_shape=[jax.ShapeDtypeStruct(shape, kind) for shape, kind in outs],
        in_specs=[vmem] * len(args),
        out_specs=[vmem] * len(outs),
        compiler_params=pltpu.CompilerParams(vmem_limit_bytes=40 * 1024 * 1024),
    )(*args)


def local(embeddings, knn_mean, pair_rows, pair_cols, pair_count, start_block):
    rows_here, width = embeddings.shape
    size = start_block.shape[0]
    slots = pair_rows.shape[2]
    lanes = lax.axis_size("cols")
    lane = lax.axis_index("cols")
    groups = lax.axis_size("rows")
    total = rows_here * groups
    assert rows_here == lanes * BLOCK and lanes == 4 and groups & (groups - 1) == 0
    wide = size + 8

    next_cells = shift(lax.dynamic_slice_in_dim(embeddings, lane * BLOCK, BLOCK, 0), 1)
    counts = jnp.pad(pair_count, ((0, 0), (0, slots - 1)))
    mine = jnp.concatenate([pair_rows[0], pair_cols[0], counts], axis=0)
    mean, left = call(
        functools.partial(vector_kernel, lanes),
        [((1, rows_here), f32), ((lanes, size + ONES, BLOCK), bf16)],
        knn_mean.reshape(rows_here // 128, 128),
        start_block,
    )
    side, masks = call(
        functools.partial(prep_kernel, lanes),
        [((size + ONES, BLOCK), bf16), ((2 * lanes, BLOCK), f32)],
        mean,
        left,
        *lane_swaps(mine),
    )
    next_side = shift(side, 1)

    unit, own_weights, own_product = call(
        functools.partial(own_kernel, lanes),
        [
            ((lanes, BLOCK, width), bf16),
            ((lanes, BLOCK, BLOCK), bf16),
            ((lanes, wide, BLOCK), f32),
        ],
        embeddings,
        mean,
        left,
    )
    (scores,) = call(
        functools.partial(scores_kernel, lanes), [((lanes, BLOCK, BLOCK), f32)], unit, next_cells
    )
    next_weights, keep, *core, back = call(
        functools.partial(next_kernel, lanes),
        [((lanes, BLOCK, BLOCK), bf16), ((lanes // 2, wide, BLOCK), f32)]
        + [((wide, BLOCK), f32)] * (lanes // 2 + 1),
        scores,
        next_side,
        mean,
        left,
        own_product,
        masks,
    )

    came = [swap(part, "cols", 1) for part in core]
    own, away = call(pair_kernel, [((wide, BLOCK), f32)] * 2, keep, *came)
    lead, smooth, wider = call(
        functools.partial(smooth_kernel, size),
        [((size, BLOCK), f32), ((wide, BLOCK), f32), ((wide + 8, BLOCK), f32)],
        own,
        swap(away, "cols", 2),
        shift(back, -1),
    )

    after = shift(wider, 1)
    across = swap(smooth, "cols", 2)
    back, gram = call(
        functools.partial(back_kernel, lanes, total),
        [((wide, BLOCK), f32), ((size, size), f32)],
        next_weights,
        next_side,
        lead,
        swap(lead, "cols", 1),
        across,
        swap(across, "cols", 1),
    )
    masks, gram = lax.optimization_barrier((masks, gram))
    keep, *core = call(
        functools.partial(forward_kernel, lanes),
        [((lanes // 2, size, BLOCK), f32)] + [((size, BLOCK), f32)] * (lanes // 2),
        own_weights,
        next_weights,
        masks,
        lead,
        after,
    )
    came = [swap(part, "cols", 1) for part in core]
    (both,) = call(chip_kernel, [(keep.shape, f32)], keep, shift(back, -1, around=False), *came)
    tall = [((size // 2 + 8 + 8 * k, 2 * size), f32) for k in range(3)]
    here, *grams = call(
        functools.partial(resmooth_kernel, total),
        [((lanes // 2, size, BLOCK), f32), *tall],
        gram,
        both,
        swap(both, "cols", 2),
        smooth,
        across,
    )

    bits = groups.bit_length() - 1
    low = bits % 2
    parts = [grams[0], swap(grams[0], "cols", 1)]
    if low:
        parts += [swap(grams[1], "rows", 1), both_swap(grams[2], 1, 1)]
    while low < bits:
        grams = call(functools.partial(sum_kernel, len(parts)), tall, *parts)
        if low < 2:
            here, grams = lax.optimization_barrier((here, grams))
        parts = [grams[0]] + [swap(grams[m - 1], "rows", m << low) for m in (1, 2, 3)]
        low += 2
    (vector,) = call(
        functools.partial(solve_kernel, lanes),
        [((size, rows_here), f32)],
        here,
        swap(here, "cols", 1),
        *parts,
    )
    return vector


def solution(mesh):
    in_specs = (
        P("rows", None),
        P("rows"),
        P("rows", "cols", None),
        P("rows", "cols", None),
        P("rows", "cols"),
        P(None, "rows"),
    )
    out_specs = P(None, "rows")
    return jax.shard_map(local, mesh=mesh, in_specs=in_specs, out_specs=out_specs, check_vma=False)
```

```python
import functools
import math

import jax
import jax.numpy as jnp
from jax import lax
from jax.experimental import pallas as pl
from jax.experimental.pallas import tpu as pltpu
from jax.sharding import PartitionSpec as P

BLOCK = 256
ONES = 16

sharpness = 10.0
epsilon = 1e-06

HIGHEST = lax.Precision.HIGHEST
f32 = jnp.float32
bf16 = jnp.bfloat16


def shift(cells, step, around=True):
    count = lax.axis_size("rows")
    pairs = [(i, (i + step) % count) for i in range(count) if around or 0 <= i + step < count]
    return lax.ppermute(cells, "rows", pairs)


def swap(cells, axis, offset):
    count = lax.axis_size(axis)
    return lax.ppermute(cells, axis, [(i, i ^ offset) for i in range(count)])


def lane_swaps(cells):
    return [cells] + [swap(cells, "cols", d) for d in range(1, lax.axis_size("cols"))]


def both_swap(cells, row_offset, lane_offset):
    groups, lanes = lax.axis_size("rows"), lax.axis_size("cols")
    pairs = [
        (r * lanes + lane, (r ^ row_offset) * lanes + (lane ^ lane_offset))
        for r in range(groups)
        for lane in range(lanes)
    ]
    return lax.ppermute(cells, ("rows", "cols"), pairs)


def nt(left, right):
    return lax.dot_general(left, right, (((1,), (1,)), ((), ())), preferred_element_type=f32)


def unit_rows(cells):
    values = cells.astype(f32)
    scale = lax.rsqrt(jnp.mean(values * values, axis=1, keepdims=True) + epsilon)
    return (values * (scale * (1.0 / math.sqrt(cells.shape[1])))).astype(bf16)


def diagonal(size):
    return lax.broadcasted_iota(jnp.int32, (size, size), 0) == lax.broadcasted_iota(
        jnp.int32, (size, size), 1
    )


def upright(row, eye):
    return jnp.sum(jnp.where(eye, row, 0.0), axis=1, keepdims=True)


def affinity(col_unit, row_unit, col_mean, row_mean):
    scores = nt(col_unit, row_unit)
    return jnp.exp((2.0 * sharpness) * scores / (col_mean + row_mean))


def weighted(scores, col_mean, row_mean):
    return jnp.exp((2.0 * sharpness) * scores / (col_mean + row_mean)).astype(bf16)


def with_ones(narrow):
    return jnp.concatenate([narrow, jnp.ones((ONES, narrow.shape[1]), bf16)], axis=0)


def pieces(values):
    first = values.astype(bf16)
    return jnp.concatenate([first, (values - first.astype(f32)).astype(bf16)], axis=0)


def joined(product, size):
    return product[:size] + product[size:]


def inverse_factor(gram):
    size = gram.shape[0]
    tile, step = 8, 4
    count = size // tile
    eye = jnp.where(diagonal(size), 1.0, 0.0).astype(f32)
    table = jnp.concatenate([gram, eye], axis=1)
    parts = [table[g * tile : (g + 1) * tile] for g in range(count)]
    shape = (tile, 2 * size)
    place = lax.broadcasted_iota(jnp.int32, shape, 0)

    def wide(piece):
        return jnp.broadcast_to(piece, shape)

    def spread(first):
        return [
            {g: wide(parts[g][:, k : k + 1]) for g in range(k // tile, count)}
            for k in range(first, min(first + step, size))
        ]

    scales = [jnp.ones(shape, f32) for _ in range(count)]
    columns = spread(0) + spread(step)
    for first in range(0, size, step):
        for t in range(step):
            b, at = (first + t) // tile, (first + t) % tile
            scale = lax.rsqrt(wide(columns[t][b][at : at + 1]))
            scales[b] = jnp.where(place == at, scale, scales[b])
            factor = {g: column * scale for g, column in columns[t].items()}
            for u in range(t + 1, len(columns)):
                g, r = (first + u) // tile, (first + u) % tile
                ahead = wide(columns[t][g][r : r + 1]) * scale
                columns[u] = {g: c - factor[g] * ahead for g, c in columns[u].items()}
            factor[b] = jnp.where(place > at, factor[b], 0.0)
            row = wide(parts[b][at : at + 1]) * scale
            for g in range(b, count):
                parts[g] = parts[g] - factor[g] * row
        columns = columns[step:] + spread(first + 2 * step)
    return jnp.concatenate([(p * s)[:, size:] for p, s in zip(parts, scales)], axis=0)


def times(left, right):
    return jnp.dot(left, right, precision=HIGHEST, preferred_element_type=f32)


def gram_of(blocks, total):
    acc = None
    for block in blocks:
        term = lax.dot_general(
            block, block, (((1,), (1,)), ((), ())), precision=HIGHEST, preferred_element_type=f32
        )
        acc = term if acc is None else acc + term
    return acc * (1.0 / total)


def block_of(lane, d):
    return pl.ds(pl.multiple_of((lane ^ d) * BLOCK, BLOCK), BLOCK)


def vector_kernel(lanes, knn_ref, start_ref, mean_ref, left_ref):
    lane = lax.axis_index("cols")
    knn = knn_ref[...].astype(f32)
    mean_ref[...] = jnp.concatenate([knn[k : k + 1] for k in range(knn.shape[0])], axis=1)
    for d in range(lanes):
        left_ref[d] = with_ones(start_ref[:, block_of(lane, d)].astype(bf16))


def prep_kernel(lanes, mean_ref, left_ref, *refs):
    lists, (side_ref, mask_ref) = refs[:lanes], refs[lanes:]
    lane = lax.axis_index("cols")
    group = lax.axis_index("rows")
    blocks = lax.axis_size("rows") * lanes
    size = left_ref.shape[1] - ONES
    stride = 4 * blocks
    codes = jnp.concatenate([ref[0:1] * stride + ref[1:2] for ref in lists], axis=0)

    def live(row_block, col_block):
        hit = jnp.where(codes == row_block * stride + col_block, 1.0, 0.0)
        hit = jnp.max(jnp.max(hit, axis=1, keepdims=True), axis=0, keepdims=True)
        return jnp.broadcast_to(hit, (1, BLOCK))

    mine = group * lanes + lane
    rows = [group * lanes + (lane ^ d) for d in range(lanes)]
    masks = [live(row, mine) for row in rows] + [live(row, mine - lanes) for row in rows]
    mask_ref[...] = jnp.concatenate(masks, axis=0)
    back = [live(mine, row + lanes) for row in rows]
    means = mean_ref[:, block_of(lane, 0)]
    pad = jnp.zeros((ONES - lanes - 1, BLOCK), f32)
    after = jnp.concatenate([means, *back, pad], axis=0).astype(bf16)
    side_ref[...] = jnp.concatenate([left_ref[0, :size, :], after], axis=0)


def own_kernel(lanes, cells_ref, mean_ref, left_ref, unit_ref, weight_ref, product_ref):
    lane = lax.axis_index("cols")
    eye = diagonal(BLOCK)
    col_mean = upright(mean_ref[:, block_of(lane, 0)], eye)
    left = left_ref[0]
    rows = product_ref.shape[1]
    for d in range(lanes):
        unit = unit_rows(cells_ref[block_of(lane, d), :])
        unit_ref[d] = unit
        if d == 0:
            own = unit
        weights = affinity(own, unit, col_mean, mean_ref[:, block_of(lane, d)])
        if d == 0:
            weights = jnp.where(eye, 0.0, weights)
        weights = weights.astype(bf16)
        weight_ref[d] = weights
        product_ref[d] = jnp.dot(left, weights, preferred_element_type=f32)[:rows]


def scores_kernel(lanes, unit_ref, cells_ref, scores_ref):
    col_unit = unit_rows(cells_ref[...])
    for d in range(lanes):
        scores_ref[d] = nt(col_unit, unit_ref[d])


def next_kernel(lanes, *refs):
    scores_ref, side_ref, mean_ref, left_ref, own_ref, mask_ref, *outs = refs
    weight_ref, keep_ref, *core_refs, back_ref = outs
    lane = lax.axis_index("cols")
    size = left_ref.shape[1] - ONES
    after = side_ref[size:, :].astype(f32)
    col_mean = upright(after[0:1], diagonal(BLOCK))
    left = with_ones(side_ref[:size, :])
    rows = own_ref.shape[1]
    back = jnp.zeros((rows, BLOCK), f32)
    for d in range(lanes):
        weights = weighted(scores_ref[d], col_mean, mean_ref[:, block_of(lane, d)])
        weight_ref[d] = weights
        product = jnp.dot(left, weights, preferred_element_type=f32)[:rows]
        own = mask_ref[d : d + 1, :] * own_ref[d]
        halves(d, keep_ref, core_refs)[...] = own + mask_ref[lanes + d : lanes + d + 1, :] * product
        back = back + after[1 + d : 2 + d] * nt(left_ref[d], weights)[:rows]
    back_ref[...] = back


def halves(d, keep_ref, core_refs):
    return core_refs[d // 2] if d % 2 else keep_ref.at[d // 2]


def added(refs):
    total = refs[0][...]
    for ref in refs[1:]:
        total = total + ref[...]
    return total


def chip_kernel(keep_ref, back_ref, *refs):
    *came_refs, out_ref = refs
    rows = out_ref.shape[1]
    for m, came_ref in enumerate(came_refs):
        total = keep_ref[m] + came_ref[...]
        out_ref[m] = total + back_ref[:rows] if m == 0 else total


def pair_kernel(keep_ref, *refs):
    *came_refs, own_ref, away_ref = refs
    own_ref[...] = keep_ref[0] + came_refs[0][...]
    away_ref[...] = keep_ref[1] + came_refs[1][...]


def smooth_kernel(size, *refs):
    *parts, lead_ref, out_ref, wide_ref = refs
    total = added(parts)
    degree = total[size : size + 1]
    smooth = total[:size] / degree
    lead_ref[...] = smooth
    out_ref[:size] = smooth
    out_ref[size:] = jnp.broadcast_to(degree, (out_ref.shape[0] - size, BLOCK))
    wide_ref[:size] = smooth
    wide_ref[size:] = jnp.zeros((wide_ref.shape[0] - size, BLOCK), f32)


def back_kernel(lanes, total, weight_ref, side_ref, *refs):
    *block_refs, back_ref, gram_ref = refs
    size = gram_ref.shape[0]
    blocks = [ref[:size] for ref in block_refs]
    masks = side_ref[size:, :].astype(f32)
    back = jnp.zeros((size, BLOCK), f32)
    for d in range(lanes):
        left = pieces(blocks[d])
        back = back + masks[1 + d : 2 + d] * joined(nt(left, weight_ref[d]), size)
    back_ref[:size] = back
    back_ref[size:] = jnp.zeros((back_ref.shape[0] - size, BLOCK), f32)
    gram_ref[...] = gram_of(blocks[::2], total)


def ordered(here_ref, there_ref):
    return [ref[m] for m in range(here_ref.shape[0]) for ref in (here_ref, there_ref)]


def forward_kernel(lanes, own_ref, weight_ref, mask_ref, lead_ref, next_ref, keep_ref, *core_refs):
    size = lead_ref.shape[0]
    own_left = pieces(lead_ref[...])
    next_left = pieces(next_ref[:size])
    for d in range(lanes):
        own = joined(jnp.dot(own_left, own_ref[d], preferred_element_type=f32), size)
        after = joined(jnp.dot(next_left, weight_ref[d], preferred_element_type=f32), size)
        own = mask_ref[d : d + 1, :] * own
        halves(d, keep_ref, core_refs)[...] = own + mask_ref[lanes + d : lanes + d + 1, :] * after


def resmooth_kernel(total, first_ref, own_ref, came_ref, block_ref, across_ref, out_ref, *grams_refs):
    size = out_ref.shape[1]
    blocks = []
    for m, ref in enumerate((block_ref, across_ref)):
        blocks.append((own_ref[m] + came_ref[1 - m]) / ref[size : size + 1])
        out_ref[m] = blocks[m]
    spread_out(packed(first_ref[...], gram_of(blocks, total)), grams_refs)


def places(size):
    shape = (size, size)
    return lax.broadcasted_iota(jnp.int32, shape, 0), lax.broadcasted_iota(jnp.int32, shape, 1)


def packed(first, second):
    size = first.shape[0]
    row, column = places(size)
    mixed = jnp.where(row >= column, first, second)
    middle = size // 2
    edge = jnp.sum(jnp.where(row == column, second, 0.0), axis=0, keepdims=True)
    edge = jnp.broadcast_to(jnp.concatenate([edge, edge], axis=1), (8, 2 * size))
    return jnp.concatenate(
        [jnp.concatenate([mixed[:middle], mixed[middle:]], axis=1), edge], axis=0
    )


def unpacked(rows, size):
    row, column = places(size)
    middle = size // 2
    mixed = jnp.concatenate([rows[:middle, :size], rows[:middle, size:]], axis=0)
    flipped = mixed.T
    first = jnp.where(row >= column, mixed, flipped)
    second = jnp.where(row < column, mixed, flipped)
    return first, jnp.where(row == column, rows[middle : middle + 1, :size], second)


def spread_out(value, refs):
    rows = value.shape[0]
    for ref in refs:
        ref[:rows] = value
        if ref.shape[0] > rows:
            ref[rows:] = jnp.zeros((ref.shape[0] - rows, ref.shape[1]), f32)


def sum_kernel(count, *refs):
    parts, outs = refs[:count], refs[count:]
    rows = outs[0].shape[0]
    total = parts[0][:rows]
    for part in parts[1:]:
        total = total + part[:rows]
    spread_out(total, outs)


def solve_kernel(lanes, here_ref, there_ref, *refs):
    *grams, out_ref = refs
    lane = lax.axis_index("cols")
    size = out_ref.shape[0]
    rows = grams[0].shape[0]
    both = grams[0][...]
    for part in grams[1:]:
        both = both + part[:rows]
    one, two = unpacked(both, size)
    first = inverse_factor(one)
    solved = [times(first, block) for block in ordered(here_ref, there_ref)]
    half = times(first, two)
    gram = lax.dot_general(
        half, first, (((1,), (1,)), ((), ())), precision=HIGHEST, preferred_element_type=f32
    )
    second = inverse_factor(gram)
    for d in range(lanes):
        out_ref[:, block_of(lane, d)] = times(second, solved[d])


def call(body, outs, *args):
    vmem = pl.BlockSpec(memory_space=pltpu.VMEM)
    return pl.pallas_call(
        body,
        out_shape=[jax.ShapeDtypeStruct(shape, kind) for shape, kind in outs],
        in_specs=[vmem] * len(args),
        out_specs=[vmem] * len(outs),
        compiler_params=pltpu.CompilerParams(vmem_limit_bytes=40 * 1024 * 1024),
    )(*args)


def local(embeddings, knn_mean, pair_rows, pair_cols, pair_count, start_block):
    rows_here, width = embeddings.shape
    size = start_block.shape[0]
    lanes = lax.axis_size("cols")
    lane = lax.axis_index("cols")
    groups = lax.axis_size("rows")
    total = rows_here * groups
    assert rows_here == lanes * BLOCK and lanes == 4 and groups & (groups - 1) == 0
    wide = size + 8

    next_cells = shift(lax.dynamic_slice_in_dim(embeddings, lane * BLOCK, BLOCK, 0), 1)
    mine = jnp.concatenate([pair_rows[0], pair_cols[0]], axis=0)
    mean, left = call(
        functools.partial(vector_kernel, lanes),
        [((1, rows_here), f32), ((lanes, size + ONES, BLOCK), bf16)],
        knn_mean.reshape(rows_here // 128, 128),
        start_block,
    )
    side, masks = call(
        functools.partial(prep_kernel, lanes),
        [((size + ONES, BLOCK), bf16), ((2 * lanes, BLOCK), f32)],
        mean,
        left,
        *lane_swaps(mine),
    )
    next_side = shift(side, 1)

    unit, own_weights, own_product = call(
        functools.partial(own_kernel, lanes),
        [
            ((lanes, BLOCK, width), bf16),
            ((lanes, BLOCK, BLOCK), bf16),
            ((lanes, wide, BLOCK), f32),
        ],
        embeddings,
        mean,
        left,
    )
    (scores,) = call(
        functools.partial(scores_kernel, lanes), [((lanes, BLOCK, BLOCK), f32)], unit, next_cells
    )
    next_weights, keep, *core, back = call(
        functools.partial(next_kernel, lanes),
        [((lanes, BLOCK, BLOCK), bf16), ((lanes // 2, wide, BLOCK), f32)]
        + [((wide, BLOCK), f32)] * (lanes // 2 + 1),
        scores,
        next_side,
        mean,
        left,
        own_product,
        masks,
    )

    came = [swap(part, "cols", 1) for part in core]
    own, away = call(pair_kernel, [((wide, BLOCK), f32)] * 2, keep, *came)
    lead, smooth, wider = call(
        functools.partial(smooth_kernel, size),
        [((size, BLOCK), f32), ((wide, BLOCK), f32), ((wide + 8, BLOCK), f32)],
        own,
        swap(away, "cols", 2),
        shift(back, -1),
    )

    after = shift(wider, 1)
    across = swap(smooth, "cols", 2)
    back, gram = call(
        functools.partial(back_kernel, lanes, total),
        [((wide, BLOCK), f32), ((size, size), f32)],
        next_weights,
        next_side,
        lead,
        swap(lead, "cols", 1),
        across,
        swap(across, "cols", 1),
    )
    masks, gram = lax.optimization_barrier((masks, gram))
    keep, *core = call(
        functools.partial(forward_kernel, lanes),
        [((lanes // 2, size, BLOCK), f32)] + [((size, BLOCK), f32)] * (lanes // 2),
        own_weights,
        next_weights,
        masks,
        lead,
        after,
    )
    came = [swap(part, "cols", 1) for part in core]
    (both,) = call(chip_kernel, [(keep.shape, f32)], keep, shift(back, -1, around=False), *came)
    tall = [((size // 2 + 8 + 8 * k, 2 * size), f32) for k in range(3)]
    here, *grams = call(
        functools.partial(resmooth_kernel, total),
        [((lanes // 2, size, BLOCK), f32), *tall],
        gram,
        both,
        swap(both, "cols", 2),
        smooth,
        across,
    )

    bits = groups.bit_length() - 1
    low = bits % 2
    parts = [grams[0], swap(grams[0], "cols", 1)]
    if low:
        parts += [swap(grams[1], "rows", 1), both_swap(grams[2], 1, 1)]
    while low < bits:
        grams = call(functools.partial(sum_kernel, len(parts)), tall, *parts)
        if low < 2:
            here, grams = lax.optimization_barrier((here, grams))
        parts = [grams[0]] + [swap(grams[m - 1], "rows", m << low) for m in (1, 2, 3)]
        low += 2
    (vector,) = call(
        functools.partial(solve_kernel, lanes),
        [((size, rows_here), f32)],
        here,
        swap(here, "cols", 1),
        *parts,
    )
    return vector


def solution(mesh):
    in_specs = (
        P("rows", None),
        P("rows"),
        P("rows", "cols", None),
        P("rows", "cols", None),
        P("rows", "cols"),
        P(None, "rows"),
    )
    out_specs = P(None, "rows")
    return jax.shard_map(local, mesh=mesh, in_specs=in_specs, out_specs=out_specs, check_vma=False)
```

```python
import functools
import math

import jax
import jax.numpy as jnp
from jax import lax
from jax.experimental import pallas as pl
from jax.experimental.pallas import tpu as pltpu
from jax.sharding import PartitionSpec as P

BLOCK = 256
ONES = 16

sharpness = 10.0
epsilon = 1e-06

HIGHEST = lax.Precision.HIGHEST
f32 = jnp.float32
bf16 = jnp.bfloat16


def shift(cells, step, around=True):
    count = lax.axis_size("rows")
    pairs = [(i, (i + step) % count) for i in range(count) if around or 0 <= i + step < count]
    return lax.ppermute(cells, "rows", pairs)


def swap(cells, axis, offset):
    count = lax.axis_size(axis)
    return lax.ppermute(cells, axis, [(i, i ^ offset) for i in range(count)])


def lane_swaps(cells):
    return [cells] + [swap(cells, "cols", d) for d in range(1, lax.axis_size("cols"))]


def both_swap(cells, row_offset, lane_offset):
    groups, lanes = lax.axis_size("rows"), lax.axis_size("cols")
    pairs = [
        (r * lanes + lane, (r ^ row_offset) * lanes + (lane ^ lane_offset))
        for r in range(groups)
        for lane in range(lanes)
    ]
    return lax.ppermute(cells, ("rows", "cols"), pairs)


def nt(left, right):
    return lax.dot_general(left, right, (((1,), (1,)), ((), ())), preferred_element_type=f32)


def unit_rows(cells):
    values = cells.astype(f32)
    scale = lax.rsqrt(jnp.mean(values * values, axis=1, keepdims=True) + epsilon)
    return (values * (scale * (1.0 / math.sqrt(cells.shape[1])))).astype(bf16)


def diagonal(size):
    return lax.broadcasted_iota(jnp.int32, (size, size), 0) == lax.broadcasted_iota(
        jnp.int32, (size, size), 1
    )


def upright(row, eye):
    return jnp.sum(jnp.where(eye, row, 0.0), axis=1, keepdims=True)


def affinity(col_unit, row_unit, col_mean, row_mean):
    scores = nt(col_unit, row_unit)
    return jnp.exp((2.0 * sharpness) * scores / (col_mean + row_mean))


def weighted(scores, col_mean, row_mean):
    return jnp.exp((2.0 * sharpness) * scores / (col_mean + row_mean)).astype(bf16)


def with_ones(narrow):
    return jnp.concatenate([narrow, jnp.ones((ONES, narrow.shape[1]), bf16)], axis=0)


def pieces(values):
    first = values.astype(bf16)
    return jnp.concatenate([first, (values - first.astype(f32)).astype(bf16)], axis=0)


def joined(product, size):
    return product[:size] + product[size:]


def inverse_factor(gram):
    size = gram.shape[0]
    tile, step = 8, 4
    count = size // tile
    eye = jnp.where(diagonal(size), 1.0, 0.0).astype(f32)
    table = jnp.concatenate([gram, eye], axis=1)
    parts = [table[g * tile : (g + 1) * tile] for g in range(count)]
    shape = (tile, 2 * size)
    place = lax.broadcasted_iota(jnp.int32, shape, 0)

    def wide(piece):
        return jnp.broadcast_to(piece, shape)

    def spread(first):
        return [
            {g: wide(parts[g][:, k : k + 1]) for g in range(k // tile, count)}
            for k in range(first, min(first + step, size))
        ]

    scales = [jnp.ones(shape, f32) for _ in range(count)]
    columns = spread(0) + spread(step)
    for first in range(0, size, step):
        for t in range(step):
            b, at = (first + t) // tile, (first + t) % tile
            scale = lax.rsqrt(wide(columns[t][b][at : at + 1]))
            scales[b] = jnp.where(place == at, scale, scales[b])
            factor = {g: column * scale for g, column in columns[t].items()}
            for u in range(t + 1, len(columns)):
                g, r = (first + u) // tile, (first + u) % tile
                ahead = wide(columns[t][g][r : r + 1]) * scale
                columns[u] = {g: c - factor[g] * ahead for g, c in columns[u].items()}
            factor[b] = jnp.where(place > at, factor[b], 0.0)
            row = wide(parts[b][at : at + 1]) * scale
            for g in range(b, count):
                parts[g] = parts[g] - factor[g] * row
        columns = columns[step:] + spread(first + 2 * step)
    return jnp.concatenate([(p * s)[:, size:] for p, s in zip(parts, scales)], axis=0)


def times(left, right):
    return jnp.dot(left, right, precision=HIGHEST, preferred_element_type=f32)


def gram_of(blocks, total):
    acc = None
    for block in blocks:
        term = lax.dot_general(
            block, block, (((1,), (1,)), ((), ())), precision=HIGHEST, preferred_element_type=f32
        )
        acc = term if acc is None else acc + term
    return acc * (1.0 / total)


def block_of(lane, d):
    return pl.ds(pl.multiple_of((lane ^ d) * BLOCK, BLOCK), BLOCK)


def vector_kernel(lanes, knn_ref, start_ref, mean_ref, left_ref):
    lane = lax.axis_index("cols")
    knn = knn_ref[...].astype(f32)
    mean_ref[...] = jnp.concatenate([knn[k : k + 1] for k in range(knn.shape[0])], axis=1)
    for d in range(lanes):
        left_ref[d] = with_ones(start_ref[:, block_of(lane, d)].astype(bf16))


def prep_kernel(lanes, mean_ref, left_ref, *refs):
    lists, (side_ref, mask_ref) = refs[:lanes], refs[lanes:]
    lane = lax.axis_index("cols")
    group = lax.axis_index("rows")
    blocks = lax.axis_size("rows") * lanes
    size = left_ref.shape[1] - ONES
    stride = 4 * blocks
    codes = jnp.concatenate([ref[0:1] * stride + ref[1:2] for ref in lists], axis=0)

    def live(row_block, col_block):
        hit = jnp.where(codes == row_block * stride + col_block, 1.0, 0.0)
        hit = jnp.max(jnp.max(hit, axis=1, keepdims=True), axis=0, keepdims=True)
        return jnp.broadcast_to(hit, (1, BLOCK))

    mine = group * lanes + lane
    rows = [group * lanes + (lane ^ d) for d in range(lanes)]
    masks = [live(row, mine) for row in rows] + [live(row, mine - lanes) for row in rows]
    mask_ref[...] = jnp.concatenate(masks, axis=0)
    back = [live(mine, row + lanes) for row in rows]
    means = mean_ref[:, block_of(lane, 0)]
    pad = jnp.zeros((ONES - lanes - 1, BLOCK), f32)
    after = jnp.concatenate([means, *back, pad], axis=0).astype(bf16)
    side_ref[...] = jnp.concatenate([left_ref[0, :size, :], after], axis=0)


def own_kernel(lanes, cells_ref, mean_ref, left_ref, unit_ref, weight_ref, product_ref):
    lane = lax.axis_index("cols")
    eye = diagonal(BLOCK)
    col_mean = upright(mean_ref[:, block_of(lane, 0)], eye)
    left = left_ref[0]
    rows = product_ref.shape[1]
    for d in range(lanes):
        unit = unit_rows(cells_ref[block_of(lane, d), :])
        unit_ref[d] = unit
        if d == 0:
            own = unit
        weights = affinity(own, unit, col_mean, mean_ref[:, block_of(lane, d)])
        if d == 0:
            weights = jnp.where(eye, 0.0, weights)
        weights = weights.astype(bf16)
        weight_ref[d] = weights
        product_ref[d] = jnp.dot(left, weights, preferred_element_type=f32)[:rows]


def scores_kernel(lanes, unit_ref, cells_ref, scores_ref):
    col_unit = unit_rows(cells_ref[...])
    for d in range(lanes):
        scores_ref[d] = nt(col_unit, unit_ref[d])


def next_kernel(lanes, *refs):
    scores_ref, side_ref, mean_ref, left_ref, own_ref, mask_ref, *outs = refs
    weight_ref, keep_ref, *core_refs, back_ref = outs
    lane = lax.axis_index("cols")
    size = left_ref.shape[1] - ONES
    after = side_ref[size:, :].astype(f32)
    col_mean = upright(after[0:1], diagonal(BLOCK))
    left = with_ones(side_ref[:size, :])
    rows = own_ref.shape[1]
    back = jnp.zeros((rows, BLOCK), f32)
    for d in range(lanes):
        weights = weighted(scores_ref[d], col_mean, mean_ref[:, block_of(lane, d)])
        weight_ref[d] = weights
        product = jnp.dot(left, weights, preferred_element_type=f32)[:rows]
        own = mask_ref[d : d + 1, :] * own_ref[d]
        halves(d, keep_ref, core_refs)[...] = own + mask_ref[lanes + d : lanes + d + 1, :] * product
        back = back + after[1 + d : 2 + d] * nt(left_ref[d], weights)[:rows]
    back_ref[...] = back


def halves(d, keep_ref, core_refs):
    return core_refs[d // 2] if d % 2 else keep_ref.at[d // 2]


def added(refs):
    total = refs[0][...]
    for ref in refs[1:]:
        total = total + ref[...]
    return total


def chip_kernel(keep_ref, back_ref, *refs):
    *came_refs, out_ref = refs
    rows = out_ref.shape[1]
    for m, came_ref in enumerate(came_refs):
        total = keep_ref[m] + came_ref[...]
        out_ref[m] = total + back_ref[:rows] if m == 0 else total


def pair_kernel(keep_ref, *refs):
    *came_refs, own_ref, away_ref = refs
    own_ref[...] = keep_ref[0] + came_refs[0][...]
    away_ref[...] = keep_ref[1] + came_refs[1][...]


def smooth_kernel(size, *refs):
    *parts, lead_ref, out_ref, wide_ref = refs
    total = added(parts)
    degree = total[size : size + 1]
    smooth = total[:size] / degree
    lead_ref[...] = smooth
    out_ref[:size] = smooth
    out_ref[size:] = jnp.broadcast_to(degree, (out_ref.shape[0] - size, BLOCK))
    wide_ref[:size] = smooth
    wide_ref[size:] = jnp.zeros((wide_ref.shape[0] - size, BLOCK), f32)


def back_kernel(lanes, total, weight_ref, side_ref, *refs):
    *block_refs, back_ref, gram_ref = refs
    size = gram_ref.shape[0]
    blocks = [ref[:size] for ref in block_refs]
    masks = side_ref[size:, :].astype(f32)
    back = jnp.zeros((size, BLOCK), f32)
    for d in range(lanes):
        left = pieces(blocks[d])
        back = back + masks[1 + d : 2 + d] * joined(nt(left, weight_ref[d]), size)
    back_ref[:size] = back
    back_ref[size:] = jnp.zeros((back_ref.shape[0] - size, BLOCK), f32)
    gram_ref[...] = gram_of(blocks[::2], total)


def ordered(here_ref, there_ref):
    return [ref[m] for m in range(here_ref.shape[0]) for ref in (here_ref, there_ref)]


def forward_kernel(lanes, own_ref, weight_ref, mask_ref, lead_ref, next_ref, keep_ref, *core_refs):
    size = lead_ref.shape[0]
    own_left = pieces(lead_ref[...])
    next_left = pieces(next_ref[:size])
    for d in range(lanes):
        own = joined(jnp.dot(own_left, own_ref[d], preferred_element_type=f32), size)
        after = joined(jnp.dot(next_left, weight_ref[d], preferred_element_type=f32), size)
        own = mask_ref[d : d + 1, :] * own
        halves(d, keep_ref, core_refs)[...] = own + mask_ref[lanes + d : lanes + d + 1, :] * after


def resmooth_kernel(total, first_ref, own_ref, came_ref, block_ref, across_ref, out_ref, *grams_refs):
    size = out_ref.shape[1]
    blocks = []
    for m, ref in enumerate((block_ref, across_ref)):
        blocks.append((own_ref[m] + came_ref[1 - m]) / ref[size : size + 1])
        out_ref[m] = blocks[m]
    spread_out(packed(first_ref[...], gram_of(blocks, total)), grams_refs)


def places(size):
    shape = (size, size)
    return lax.broadcasted_iota(jnp.int32, shape, 0), lax.broadcasted_iota(jnp.int32, shape, 1)


def packed(first, second):
    size = first.shape[0]
    row, column = places(size)
    mixed = jnp.where(row >= column, first, second)
    middle = size // 2
    edge = jnp.sum(jnp.where(row == column, second, 0.0), axis=0, keepdims=True)
    edge = jnp.broadcast_to(jnp.concatenate([edge, edge], axis=1), (8, 2 * size))
    return jnp.concatenate(
        [jnp.concatenate([mixed[:middle], mixed[middle:]], axis=1), edge], axis=0
    )


def unpacked(rows, size):
    row, column = places(size)
    middle = size // 2
    mixed = jnp.concatenate([rows[:middle, :size], rows[:middle, size:]], axis=0)
    flipped = mixed.T
    first = jnp.where(row >= column, mixed, flipped)
    second = jnp.where(row < column, mixed, flipped)
    return first, jnp.where(row == column, rows[middle : middle + 1, :size], second)


def spread_out(value, refs):
    rows = value.shape[0]
    for ref in refs:
        ref[:rows] = value
        if ref.shape[0] > rows:
            ref[rows:] = jnp.zeros((ref.shape[0] - rows, ref.shape[1]), f32)


def sum_kernel(count, *refs):
    parts, outs = refs[:count], refs[count:]
    rows = outs[0].shape[0]
    total = parts[0][:rows]
    for part in parts[1:]:
        total = total + part[:rows]
    spread_out(total, outs)


def solve_kernel(lanes, here_ref, there_ref, *refs):
    *grams, out_ref = refs
    lane = lax.axis_index("cols")
    size = out_ref.shape[0]
    rows = grams[0].shape[0]
    both = grams[0][...]
    for part in grams[1:]:
        both = both + part[:rows]
    one, two = unpacked(both, size)
    first = inverse_factor(one)
    solved = [times(first, block) for block in ordered(here_ref, there_ref)]
    half = times(first, two)
    gram = lax.dot_general(
        half, first, (((1,), (1,)), ((), ())), precision=HIGHEST, preferred_element_type=f32
    )
    second = inverse_factor(gram)
    for d in range(lanes):
        out_ref[:, block_of(lane, d)] = times(second, solved[d])


def call(body, outs, *args):
    vmem = pl.BlockSpec(memory_space=pltpu.VMEM)
    return pl.pallas_call(
        body,
        out_shape=[jax.ShapeDtypeStruct(shape, kind) for shape, kind in outs],
        in_specs=[vmem] * len(args),
        out_specs=[vmem] * len(outs),
        compiler_params=pltpu.CompilerParams(vmem_limit_bytes=40 * 1024 * 1024),
    )(*args)


def local(embeddings, knn_mean, pair_rows, pair_cols, pair_count, start_block):
    rows_here, width = embeddings.shape
    size = start_block.shape[0]
    lanes = lax.axis_size("cols")
    lane = lax.axis_index("cols")
    groups = lax.axis_size("rows")
    total = rows_here * groups
    assert rows_here == lanes * BLOCK and lanes == 4 and groups & (groups - 1) == 0
    wide = size + 8

    next_cells = shift(lax.dynamic_slice_in_dim(embeddings, lane * BLOCK, BLOCK, 0), 1)
    mine = jnp.concatenate([pair_rows[0], pair_cols[0]], axis=0)
    mean, left = call(
        functools.partial(vector_kernel, lanes),
        [((1, rows_here), f32), ((lanes, size + ONES, BLOCK), bf16)],
        knn_mean.reshape(rows_here // 128, 128),
        start_block,
    )
    side, masks = call(
        functools.partial(prep_kernel, lanes),
        [((size + ONES, BLOCK), bf16), ((2 * lanes, BLOCK), f32)],
        mean,
        left,
        *lane_swaps(mine),
    )
    next_side = shift(side, 1)

    unit, own_weights, own_product = call(
        functools.partial(own_kernel, lanes),
        [
            ((lanes, BLOCK, width), bf16),
            ((lanes, BLOCK, BLOCK), bf16),
            ((lanes, wide, BLOCK), f32),
        ],
        embeddings,
        mean,
        left,
    )
    (scores,) = call(
        functools.partial(scores_kernel, lanes), [((lanes, BLOCK, BLOCK), f32)], unit, next_cells
    )
    next_weights, keep, *core, back = call(
        functools.partial(next_kernel, lanes),
        [((lanes, BLOCK, BLOCK), bf16), ((lanes // 2, wide, BLOCK), f32)]
        + [((wide, BLOCK), f32)] * (lanes // 2 + 1),
        scores,
        next_side,
        mean,
        left,
        own_product,
        masks,
    )

    came = [swap(part, "cols", 1) for part in core]
    own, away = call(pair_kernel, [((wide, BLOCK), f32)] * 2, keep, *came)
    lead, smooth, wider = call(
        functools.partial(smooth_kernel, size),
        [((size, BLOCK), f32), ((wide, BLOCK), f32), ((wide + 8, BLOCK), f32)],
        own,
        swap(away, "cols", 2),
        shift(back, -1),
    )

    after = shift(wider, 1)
    across = swap(smooth, "cols", 2)
    back, gram = call(
        functools.partial(back_kernel, lanes, total),
        [((wide, BLOCK), f32), ((size, size), f32)],
        next_weights,
        next_side,
        lead,
        swap(lead, "cols", 1),
        across,
        swap(across, "cols", 1),
    )
    masks, gram = lax.optimization_barrier((masks, gram))
    keep, *core = call(
        functools.partial(forward_kernel, lanes),
        [((lanes // 2, size, BLOCK), f32)] + [((size, BLOCK), f32)] * (lanes // 2),
        own_weights,
        next_weights,
        masks,
        lead,
        after,
    )
    came = [swap(part, "cols", 1) for part in core]
    (both,) = call(chip_kernel, [(keep.shape, f32)], keep, shift(back, -1, around=False), *came)
    tall = [((size // 2 + 8 + 8 * k, 2 * size), f32) for k in range(2)]
    here, *grams = call(
        functools.partial(resmooth_kernel, total),
        [((lanes // 2, size, BLOCK), f32), *tall],
        gram,
        both,
        swap(both, "cols", 2),
        smooth,
        across,
    )

    bits = groups.bit_length() - 1
    low = bits % 2
    parts = [grams[0], swap(grams[0], "cols", 1)]
    if low:
        parts += [swap(grams[0], "rows", 1), both_swap(grams[1], 1, 1)]
    while low < bits:
        grams = call(functools.partial(sum_kernel, len(parts)), tall, *parts)
        if low < 2:
            here, grams = lax.optimization_barrier((here, grams))
        parts = [grams[0]] + [swap(grams[m // 3], "rows", m << low) for m in (1, 2, 3)]
        low += 2
    (vector,) = call(
        functools.partial(solve_kernel, lanes),
        [((size, rows_here), f32)],
        here,
        swap(here, "cols", 1),
        *parts,
    )
    return vector


def solution(mesh):
    in_specs = (
        P("rows", None),
        P("rows"),
        P("rows", "cols", None),
        P("rows", "cols", None),
        P("rows", "cols"),
        P(None, "rows"),
    )
    out_specs = P(None, "rows")
    return jax.shard_map(local, mesh=mesh, in_specs=in_specs, out_specs=out_specs, check_vma=False)
```
